32 devices in a mesh: lon: 4 (over z), lat: 2 (over x), ens: 4 (over y, core).
Axes of the slice: x: 2, y: 2, z: 4, core: 2. Of those that a mesh axis runs over, the one named last changes fastest.
Arguments:
- field: bfloat16 [4, 32, 256, 128], P('ens', 'lat', 'lon'), may hold values from -6 to 6
- cotangent: bfloat16 [4, 32, 256, 128], P('ens', 'lat', 'lon'), may hold values from -6 to 6
- land_mask: int32 [32, 256], P('lat', 'lon'), may hold values from 0 to 1, as said below
- kernel_taps: float32 [49, 128], replicated, may hold values from -0.875 to 0.875
- norm_gain: float32 [128], replicated, may hold values from 0.1 to 1.9
- norm_shift: float32 [128], replicated, may hold values from -3 to 3
- up_weight: bfloat16 [128, 256], replicated, may hold values from -0.5 to 0.5
- down_weight: bfloat16 [256, 128], replicated, may hold values from -0.375 to 0.375
Outputs:
- output: bfloat16 [4, 32, 256, 128], P('ens', 'lat', 'lon')
- field_grad: bfloat16 [4, 32, 256, 128], P('ens', 'lat', 'lon')
- kernel_grad: float32 [49, 128], replicated
- norm_grad: float32 [2, 128], replicated
- up_grad: float32 [128, 256], replicated
- down_grad: float32 [256, 128], replicated
The draws below stay inside these ranges and needn't reach their ends.
Inputs may be any that keep to these rules, and one draw needn't show every extreme that they name: `land_mask`: 1 marks an ocean cell and 0 a land cell; the share of ocean differs from tile to tile.
All inputs are finite; a program needn't handle non-finite values.
Results may differ from the reference program's by a relative error of at most 0.0062.
Values may be sent and summed in bfloat16 or wider, within the bound.
No kernel may reach another device: no remote copies, remote signals or barrier semaphores. Data moves between devices by JAX's collectives and lax.ppermute only.
A program may use at most 64 MiB of HBM per device.

```python
import math
import jax
import jax.numpy as jnp
from jax import lax

CHANNELS = 128
HIDDEN_SIZE = 256
KERNEL = 7
DILATION = 2
REACH = 6
TILE_LAT = 16
TILE_LON = 64
MEMBERS = 4
GRID_LAT = 32
GRID_LON = 256


def draw_land_mask(key, part):
    level_key = jax.random.fold_in(key, 11)
    cell_key = jax.random.fold_in(key, 23)
    levels = jax.random.randint(level_key, (GRID_LAT // TILE_LAT, GRID_LON // TILE_LON), 0, 5)
    spread = jnp.repeat(jnp.repeat(levels, TILE_LAT, 0), TILE_LON, 1)
    cells = jax.random.randint(cell_key, (GRID_LAT, GRID_LON), 0, 4)
    return (cells < spread).astype(jnp.int32)


def block_scale(rng, extent, split, least, top_value):
    def one(position, parts):
        heights = jax.random.uniform(jax.random.fold_in(jax.random.fold_in(rng, 6), position), (parts,), jnp.float32, least / len(split), top_value / len(split))
        return jnp.repeat(jnp.exp(heights), extent[position] // parts).reshape((-1,) + (1,) * (len(extent) - position - 1))

    gain = one(*split[0])
    for cut in split[1:]:
        gain = gain * one(*cut)
    return gain


def bell_draw(key, dims, width, most, shards=(), held_as=jnp.bfloat16):
    values = width * jax.random.normal(key, dims, jnp.float32)
    if shards:
        values = values * block_scale(key, dims, shards, -0.22, 0.18)
    return jnp.clip(values, -most, most).astype(held_as)


def setup_inputs(seed: int = 0) -> dict:
    arg_keys = jax.random.split(jax.random.key(seed), 9)
    return {
        "field": bell_draw(arg_keys[0], (MEMBERS, GRID_LAT, GRID_LON, CHANNELS), 1.0, 6.0, ((0, 4), (1, 2), (2, 4))),
        "cotangent": bell_draw(arg_keys[1], (MEMBERS, GRID_LAT, GRID_LON, CHANNELS), 1.0, 6.0, ((0, 4), (1, 2), (2, 4))),
        "land_mask": draw_land_mask(jax.random.fold_in(arg_keys[8], 71), 0),
        "kernel_taps": bell_draw(arg_keys[3], (KERNEL * KERNEL, CHANNELS), (KERNEL * KERNEL) ** -0.5, 0.875, (), jnp.float32),
        "norm_gain": jnp.clip(1.0 + 0.18 * jax.random.normal(arg_keys[4], (CHANNELS,), jnp.float32), 0.1, 1.9),
        "norm_shift": bell_draw(arg_keys[5], (CHANNELS,), 0.5, 3.0, (), jnp.float32),
        "up_weight": bell_draw(arg_keys[6], (CHANNELS, HIDDEN_SIZE), CHANNELS ** -0.5, 0.5),
        "down_weight": bell_draw(arg_keys[7], (HIDDEN_SIZE, CHANNELS), HIDDEN_SIZE ** -0.5, 0.375),
    }


def extend(masked):
    top_rows = masked[GRID_LAT - REACH:][::-1, ::-1]
    lower = jnp.zeros((REACH, GRID_LON, masked.shape[2]), masked.dtype)
    tall = jnp.concatenate([lower, masked, top_rows], 0)
    return jnp.concatenate([tall[:, GRID_LON - REACH:], tall, tall[:, :REACH]], 1)

def depthwise(widened, kernel_taps):
    rows = widened.shape[0] - 2 * REACH
    cols = widened.shape[1] - 2 * REACH
    total = jnp.zeros((rows, cols, widened.shape[2]), jnp.float32)
    for row_tap in range(KERNEL):
        for col_tap in range(KERNEL):
            window = widened[DILATION * row_tap:DILATION * row_tap + rows, DILATION * col_tap:DILATION * col_tap + cols]
            total = total + kernel_taps[row_tap * KERNEL + col_tap] * window
    return total

def member_pass(state, upstream_in, land_mask, kernel_taps, norm_gain, norm_shift, up_weight, down_weight):
    sea = land_mask.astype(jnp.float32)[:, :, None]
    masked = (state.astype(jnp.float32) * sea).astype(jnp.bfloat16)
    masked_wide = masked.astype(jnp.float32)
    widened, extend_back = jax.vjp(extend, masked_wide)
    mixed, conv_back = jax.vjp(depthwise, widened, kernel_taps)
    centered = mixed - lax.optimization_barrier(jnp.mean(mixed, -1, keepdims=True))
    rstd = lax.rsqrt(lax.optimization_barrier(jnp.mean(centered * centered, -1, keepdims=True)) + 1e-06)
    unit = centered * rstd
    normed = (unit * norm_gain + norm_shift).astype(jnp.bfloat16)
    cells = GRID_LAT * GRID_LON
    flat_norm = normed.reshape(cells, CHANNELS)
    pre = jnp.dot(flat_norm, up_weight, preferred_element_type=jnp.float32)
    slope = math.sqrt(2.0 / math.pi)
    tanh_val = jnp.tanh(slope * (pre + 0.044715 * pre * pre * pre))
    activated = (0.5 * pre * (1.0 + tanh_val)).astype(jnp.bfloat16)
    product = jnp.dot(activated, down_weight, preferred_element_type=jnp.float32).reshape(GRID_LAT, GRID_LON, CHANNELS)
    output = ((state.astype(jnp.float32) + product) * sea).astype(jnp.bfloat16)
    upstream = (upstream_in.astype(jnp.float32) * sea).astype(jnp.bfloat16)
    flat_up = upstream.reshape(cells, CHANNELS)
    down_part = jnp.dot(activated.T, flat_up, preferred_element_type=jnp.float32)
    act_grad = jnp.dot(flat_up, down_weight.T, preferred_element_type=jnp.float32)
    deriv = 0.5 * (1.0 + tanh_val) + 0.5 * pre * (1.0 - tanh_val * tanh_val) * slope * (1.0 + 3.0 * 0.044715 * pre * pre)
    pre_grad = (act_grad * deriv).astype(jnp.bfloat16)
    up_part = jnp.dot(flat_norm.T, pre_grad, preferred_element_type=jnp.float32)
    norm_in_grad = jnp.dot(pre_grad, up_weight.T, preferred_element_type=jnp.float32).reshape(GRID_LAT, GRID_LON, CHANNELS)
    norm_part = jnp.stack([lax.optimization_barrier(jnp.sum(norm_in_grad * unit, (0, 1))), lax.optimization_barrier(jnp.sum(norm_in_grad, (0, 1)))])
    scaled = norm_in_grad * norm_gain
    mixed_grad = rstd * (scaled - lax.optimization_barrier(jnp.mean(scaled, -1, keepdims=True)) - unit * lax.optimization_barrier(jnp.mean(scaled * unit, -1, keepdims=True)))
    extended_grad, kernel_part = conv_back(mixed_grad)
    masked_grad = extend_back(extended_grad)[0]
    field_grad = ((upstream_in.astype(jnp.float32) + masked_grad) * sea).astype(jnp.bfloat16)
    return (output, field_grad, kernel_part, norm_part, up_part, down_part)

def reference(field, cotangent, land_mask, kernel_taps, norm_gain, norm_shift, up_weight, down_weight):

    def one_member(pair):
        return member_pass(pair[0], pair[1], land_mask, kernel_taps, norm_gain, norm_shift, up_weight, down_weight)
    output, field_grad, kernel_part, norm_part, up_part, down_part = lax.map(one_member, (field, cotangent))
    factor = 1.0 / math.sqrt(MEMBERS * GRID_LAT * GRID_LON)
    return (output, field_grad, lax.optimization_barrier(jnp.sum(kernel_part, 0)) * factor, lax.optimization_barrier(jnp.sum(norm_part, 0)) * factor, lax.optimization_barrier(jnp.sum(up_part, 0)) * factor, lax.optimization_barrier(jnp.sum(down_part, 0)) * factor)
```

```python
import functools
import math

import jax
import jax.numpy as jnp
from jax import lax
from jax.experimental import pallas as pl
from jax.experimental.pallas import tpu as pltpu
from jax.sharding import PartitionSpec as P

KERNEL = 7
DILATION = 2
REACH = 6
TAPS = KERNEL * KERNEL
LANE = 8
LEFT = 8
BASE = LEFT - REACH
SLOPE = math.sqrt(2.0 / math.pi)
CUBIC = 0.044715
F32, BF16 = jnp.float32, jnp.bfloat16


def route(axes, target):
    sizes = [lax.axis_size(a) for a in axes]
    pairs = []
    for flat in range(math.prod(sizes)):
        rest, at = flat, []
        for size in reversed(sizes):
            at.append(rest % size)
            rest //= size
        at = at[::-1]
        to = target(*at)
        if to is not None:
            dest = 0
            for size, i in zip(sizes, to):
                dest = dest * size + i
            pairs.append((flat, dest))
    return pairs


def is_northern():
    return lax.axis_index("lat") == lax.axis_size("lat") - 1


def row_halos(block):
    count, width = lax.axis_size("lat"), lax.axis_size("lon")
    top, bottom = block[block.shape[0] - REACH :], block[:REACH]
    northern = is_northern()
    axes = ("lon", "lat")
    fold = route(axes, lambda c, r: (width - 1 - c, r) if r == count - 1 else None)
    folded = lax.ppermute(top[::-1, ::-1], axes, fold)
    if count == 2:
        facing = lax.ppermute(jnp.where(northern, bottom, top), "lat", [(0, 1), (1, 0)])
        south = jnp.where(northern, facing, jnp.zeros_like(facing))
        north = jnp.where(northern, folded, facing)
    else:
        south = lax.ppermute(top, "lat", [(i, i + 1) for i in range(count - 1)])
        above = lax.ppermute(bottom, "lat", [(i + 1, i) for i in range(count - 1)])
        north = jnp.where(northern, folded, above)
    return south, north


def extend(block):
    south, north = row_halos(block)
    cols = block.shape[1]
    count = lax.axis_size("lon")
    first = jnp.concatenate([a[:, :REACH] for a in (south, block, north)], 0)
    last = jnp.concatenate([a[:, cols - REACH :] for a in (south, block, north)], 0)
    west = lax.ppermute(last, "lon", [(i, (i + 1) % count) for i in range(count)])
    east = lax.ppermute(first, "lon", [((i + 1) % count, i) for i in range(count)])
    return south, block, north, west, east


def partners(value, bits):
    axes = tuple(a for a in ("lon", "lat", "ens") if a in [b[0] for b in bits])
    flip = {a: 0 for a in axes}
    for a, b in bits:
        flip[a] ^= b
    return lax.ppermute(value, axes, route(axes, lambda *at: [i ^ flip[a] for a, i in zip(axes, at)]))


def summed(packed):
    axes = ("ens", "lat", "lon")
    bits = [(a, 1 << b) for a in axes for b in range(lax.axis_size(a).bit_length() - 1)]
    if any(lax.axis_size(a) & (lax.axis_size(a) - 1) for a in axes):
        return lax.psum(packed.astype(F32), axes)
    half = packed.shape[0] // 2
    split = bits[0]
    odd = lax.axis_index(split[0]) & 1
    low, high = packed[:half], packed[half:]
    mine = jnp.where(odd == 0, low, high)
    other = jnp.where(odd == 0, high, low)
    total = mine.astype(F32) + partners(other, [split]).astype(F32)
    rest = bits[1:]
    while rest:
        pair, rest = rest[:2], rest[2:]
        sent = total.astype(BF16)
        if len(pair) == 2:
            far = partners(sent, pair)
            one, two = partners(sent, pair[:1]), partners(sent, pair[1:])
            total = (sent.astype(F32) + one.astype(F32)) + (two.astype(F32) + far.astype(F32))
        else:
            total = sent.astype(F32) + partners(sent, pair).astype(F32)
    back = partners(total, [split])
    return jnp.where(odd == 0, jnp.concatenate([total, back]), jnp.concatenate([back, total]))


def fill(wide, south, block, north, west, east):
    rows, cols = block.shape[0], block.shape[1]
    for ref, start, count in ((south, 0, REACH), (block, REACH, rows), (north, REACH + rows, REACH)):

        def one(r, carry, ref=ref, start=start):
            wide[start + r, LEFT : LEFT + cols] = ref[r].astype(F32)
            return carry

        lax.fori_loop(0, count, one, 0, unroll=2)

    def sides(r, carry):
        wide[r, BASE:LEFT] = west[r].astype(F32)
        wide[r, LEFT + cols : LEFT + cols + REACH] = east[r].astype(F32)
        return carry

    lax.fori_loop(0, rows + 2 * REACH, sides, 0, unroll=4)


def conv(wide, tap, rows, cols, store):
    lines = rows // 2
    groups = math.gcd(cols // LANE, 4)

    def parity(q, carry):
        for first in range(0, cols // LANE, groups):
            sums = [[None] * groups for _ in range(lines)]
            for k in range(lines + KERNEL - 1):
                for j in range(KERNEL):
                    at = [BASE + (first + g) * LANE + DILATION * j for g in range(groups)]
                    values = [wide[q + 2 * k, a : a + LANE] for a in at]
                    for i in range(KERNEL):
                        line = k - i
                        if 0 <= line < lines:
                            weight = tap(k, i, j)
                            for g in range(groups):
                                term = weight * values[g]
                                old = sums[line][g]
                                sums[line][g] = term if old is None else old + term
            for line in range(lines):
                for g in range(groups):
                    store(q + 2 * line, (first + g) * LANE, sums[line][g])
        return carry

    lax.fori_loop(0, 2, parity, 0)


def forward_kernel(south, block, north, west, east, upstream, sea, taps, gain, shift, up, down,
                   output, grad, packed, wide, spread, mixed):
    rows, cols, channels = block.shape
    hidden = up.shape[1]
    for k in range(TAPS):
        spread[k] = jnp.broadcast_to(taps[k : k + 1], (LANE, channels))
    fill(wide, south, block, north, west, east)

    def store(row, col, value):
        mixed[row, col : col + LANE] = value

    conv(wide, lambda k, i, j: spread[i * KERNEL + j], rows, cols, store)

    up_w, down_w = up[...], down[...]
    gain_v, shift_v = gain[...], shift[...]
    lines = 4
    cells = lines * cols
    nt = (((1,), (1,)), ((), ()))
    tn = (((0,), (0,)), ((), ()))

    def chunk(n, carry):
        up_sum, down_sum, gain_sum, shift_sum = carry
        at = pl.ds(n * lines, lines)
        value = mixed[at].reshape(cells, channels)
        centered = value - jnp.mean(value, -1, keepdims=True)
        rstd = lax.rsqrt(jnp.mean(centered * centered, -1, keepdims=True) + 1e-06)
        unit = centered * rstd
        normed = (unit * gain_v + shift_v).astype(BF16)
        pre = jnp.dot(normed, up_w, preferred_element_type=F32)
        square = pre * pre
        tanh = jnp.tanh(pre * (SLOPE + (SLOPE * CUBIC) * square))
        gate = 0.5 + 0.5 * tanh
        activated = (pre * gate).astype(BF16)
        product = jnp.dot(activated, down_w, preferred_element_type=F32)
        ocean = sea[at].reshape(cells, channels).astype(F32)
        state = block[at].reshape(cells, channels).astype(F32)
        output[at] = ((state + product) * ocean).astype(BF16).reshape(lines, cols, channels)
        above = upstream[at].reshape(cells, channels)
        down_sum = down_sum + lax.dot_general(above, activated, tn, preferred_element_type=F32)
        act_grad = lax.dot_general(above, down_w, nt, preferred_element_type=F32)
        deriv = gate + pre * (gate * (1.0 - tanh)) * (SLOPE + (3.0 * SLOPE * CUBIC) * square)
        pre_grad = (act_grad * deriv).astype(BF16)
        up_sum = up_sum + lax.dot_general(normed, pre_grad, tn, preferred_element_type=F32)
        norm_in = lax.dot_general(pre_grad, up_w, nt, preferred_element_type=F32)
        gain_sum = gain_sum + jnp.sum((norm_in * unit).reshape(cells // LANE, LANE, channels), 0)
        shift_sum = shift_sum + jnp.sum(norm_in.reshape(cells // LANE, LANE, channels), 0)
        scaled = norm_in * gain_v
        inner = jnp.mean(scaled * unit, -1, keepdims=True)
        result = rstd * (scaled - jnp.mean(scaled, -1, keepdims=True) - unit * inner)
        mixed[at] = result.reshape(lines, cols, channels)
        grad[at] = result.astype(BF16).reshape(lines, cols, channels)
        return up_sum, down_sum, gain_sum, shift_sum

    big = jnp.zeros((channels, hidden), F32)
    small = jnp.zeros((LANE, channels), F32)
    up_sum, down_sum, gain_sum, shift_sum = lax.fori_loop(
        0, rows // lines, chunk, (big, big, small, small)
    )
    packed[0:hidden] = down_sum.T.astype(BF16)
    for n in range(hidden // channels):
        start = hidden + n * channels
        packed[start : start + channels] = up_sum[:, n * channels : (n + 1) * channels].astype(BF16)

    pieces = []
    for taps_i in (range(0, 4), range(4, KERNEL)):

        def quad(n, sums, taps_i=taps_i):
            base = (n // 2) * 8 + n % 2
            sums = list(sums)
            for g in range(cols // LANE):
                grads = [mixed[base + 2 * m, g * LANE : (g + 1) * LANE] for m in range(4)]
                for k in range(taps_i[0], taps_i[-1] + 4):
                    for j in range(KERNEL):
                        a = BASE + g * LANE + DILATION * j
                        value = wide[base + 2 * k, a : a + LANE]
                        for m in range(4):
                            if k - m in taps_i:
                                at = (k - m - taps_i[0]) * KERNEL + j
                                sums[at] = sums[at] + grads[m] * value
            return tuple(sums)

        zero = tuple(small for _ in range(len(taps_i) * KERNEL))
        pieces += list(lax.fori_loop(0, rows // 4, quad, zero))
    pieces += [gain_sum, shift_sum]
    pieces = [jnp.sum(p, 0, keepdims=True) for p in pieces]
    pieces += [jnp.zeros((packed.shape[0] - 2 * hidden - len(pieces), channels), F32)]
    packed[2 * hidden :] = jnp.concatenate(pieces, 0).astype(BF16)


def backward_kernel(northern, south, block, north, west, east, upstream, sea, taps,
                    field_grad, wide, spread, folded):
    rows, cols, channels = block.shape
    for k in range(TAPS):
        flipped = jnp.broadcast_to(taps[TAPS - 1 - k : TAPS - k], (LANE, channels))
        plain = jnp.broadcast_to(taps[k : k + 1], (LANE, channels))
        spread[k] = flipped
        folded[k] = jnp.where(northern[0] == 1, plain, flipped)
    fill(wide, south, block, north, west, east)
    edge = (REACH + rows) // 2

    def tap(k, i, j):
        return (folded if k >= edge else spread)[i * KERNEL + j]

    def store(row, col, value):
        at = (row, slice(col, col + LANE))
        field_grad[at] = ((upstream[at].astype(F32) + value) * sea[at].astype(F32)).astype(BF16)

    conv(wide, tap, rows, cols, store)


def shards(field, cotangent, land_mask, kernel_taps, norm_gain, norm_shift, up_weight, down_weight):
    rows, cols, channels = field.shape[1:]
    hidden = up_weight.shape[1]
    sea = jnp.broadcast_to(land_mask.astype(BF16)[:, :, None], (rows, cols, channels))
    masked = field[0] * sea
    upstream = cotangent[0] * sea
    vmem = pl.BlockSpec(memory_space=pltpu.VMEM)
    smem = pl.BlockSpec(memory_space=pltpu.SMEM)
    wide = pltpu.VMEM((rows + 2 * REACH, cols + 2 * LEFT, channels), F32)
    spread = pltpu.VMEM((TAPS, LANE, channels), F32)
    small = -(-(TAPS + 2) // 64) * 64
    macs = TAPS * rows * cols * channels
    output, grad, packed = pl.pallas_call(
        forward_kernel,
        out_shape=(
            jax.ShapeDtypeStruct((rows, cols, channels), BF16),
            jax.ShapeDtypeStruct((rows, cols, channels), BF16),
            jax.ShapeDtypeStruct((2 * hidden + small, channels), BF16),
        ),
        in_specs=[vmem] * 12,
        out_specs=[vmem] * 3,
        scratch_shapes=[wide, spread, pltpu.VMEM((rows, cols, channels), F32)],
        compiler_params=pltpu.CompilerParams(vmem_limit_bytes=32 * 1024 * 1024),
        cost_estimate=pl.CostEstimate(flops=100 * macs, bytes_accessed=3 << 20, transcendentals=0),
        name="forward",
    )(*extend(masked), upstream, sea, kernel_taps, norm_gain[None], norm_shift[None], up_weight, down_weight)

    northern = is_northern().astype(jnp.int32)[None]
    field_grad = pl.pallas_call(
        backward_kernel,
        out_shape=jax.ShapeDtypeStruct((rows, cols, channels), BF16),
        in_specs=[smem] + [vmem] * 8,
        out_specs=vmem,
        scratch_shapes=[wide, spread, spread],
        compiler_params=pltpu.CompilerParams(vmem_limit_bytes=32 * 1024 * 1024),
        cost_estimate=pl.CostEstimate(flops=40 * macs, bytes_accessed=2 << 20, transcendentals=0),
        name="backward",
    )(northern, *extend(grad), upstream, sea, kernel_taps)

    count = rows * cols * lax.axis_size("lon") * lax.axis_size("lat") * lax.axis_size("ens")
    total = summed(packed) * (1.0 / math.sqrt(count))
    down_grad = total[:hidden]
    up_grad = jnp.concatenate(
        [total[hidden + n * channels : hidden + (n + 1) * channels] for n in range(hidden // channels)], 1
    )
    kernel_grad = total[2 * hidden : 2 * hidden + TAPS]
    norm_grad = total[2 * hidden + TAPS : 2 * hidden + TAPS + 2]
    return output[None], field_grad[None], kernel_grad, norm_grad, up_grad, down_grad


def solution(mesh):
    grid = P("ens", "lat", "lon", None)
    return jax.shard_map(
        shards,
        mesh=mesh,
        in_specs=(grid, grid, P("lat", "lon"), P(), P(), P(), P(), P()),
        out_specs=(grid, grid, P(), P(), P(), P()),
        check_vma=False,
    )
```

```python
import functools
import math

import jax
import jax.numpy as jnp
from jax import lax
from jax.experimental import pallas as pl
from jax.experimental.pallas import tpu as pltpu
from jax.sharding import PartitionSpec as P

KERNEL = 7
DILATION = 2
REACH = 6
TAPS = KERNEL * KERNEL
LANE = 8
LEFT = 8
BASE = LEFT - REACH
SLOPE = math.sqrt(2.0 / math.pi)
CUBIC = 0.044715
F32, BF16 = jnp.float32, jnp.bfloat16


def route(axes, target):
    sizes = [lax.axis_size(a) for a in axes]
    pairs = []
    for flat in range(math.prod(sizes)):
        rest, at = flat, []
        for size in reversed(sizes):
            at.append(rest % size)
            rest //= size
        at = at[::-1]
        to = target(*at)
        if to is not None:
            dest = 0
            for size, i in zip(sizes, to):
                dest = dest * size + i
            pairs.append((flat, dest))
    return pairs


def is_northern():
    return lax.axis_index("lat") == lax.axis_size("lat") - 1


def xor_partner(value, axis, bits):
    return lax.ppermute(value, axis, [(i, i ^ bits) for i in range(lax.axis_size(axis))])


def columns(block, top):
    count = lax.axis_size("lon")
    first, last = block[:, :REACH], block[:, block.shape[1] - REACH :]
    flipped = top[::-1, ::-1]
    if count == 4:
        even = lax.axis_index("lon") % 2 == 0
        near, far = jnp.where(even, last, first), jnp.where(even, first, last)
        corner = jnp.where(even, flipped[:, :REACH], flipped[:, flipped.shape[1] - REACH :])
        own = jnp.where(even, flipped[:, flipped.shape[1] - REACH :], flipped[:, :REACH])
        channels = block.shape[2]
        cells = far.shape[0] * far.shape[1]
        joint = jnp.concatenate([far.reshape(-1, channels), flipped.reshape(-1, channels)])
        joint = xor_partner(joint, "lon", 3)
        corner = xor_partner(corner, "lon", 2)
        near = xor_partner(near, "lon", 1)
        far, folded = joint[:cells].reshape(far.shape), joint[cells:].reshape(flipped.shape)
        west, east = jnp.where(even, far, near), jnp.where(even, near, far)
        sides = [jnp.where(even, own, corner), folded, jnp.where(even, corner, own)]
        return west, east, jnp.concatenate(sides, 1)
    ring = [(i, (i + 1) % count) for i in range(count)]
    back = [(j, i) for i, j in ring]
    folded = lax.ppermute(flipped, "lon", [(i, count - 1 - i) for i in range(count)])
    west, east = lax.ppermute(last, "lon", ring), lax.ppermute(first, "lon", back)
    left = lax.ppermute(folded[:, folded.shape[1] - REACH :], "lon", ring)
    right = lax.ppermute(folded[:, :REACH], "lon", back)
    return west, east, jnp.concatenate([left, folded, right], 1)


def extend(block):
    count = lax.axis_size("lat")
    top, bottom = block[block.shape[0] - REACH :], block[:REACH]
    west, east, folded = columns(block, top)
    northern = is_northern()
    top = jnp.concatenate([west[-REACH:], top, east[-REACH:]], 1)
    bottom = jnp.concatenate([west[:REACH], bottom, east[:REACH]], 1)
    if count == 2:
        facing = xor_partner(jnp.where(northern, bottom, top), "lat", 1)
        south = jnp.where(northern, facing, jnp.zeros_like(facing))
        north = jnp.where(northern, folded, facing)
    else:
        south = lax.ppermute(top, "lat", [(i, i + 1) for i in range(count - 1)])
        above = lax.ppermute(bottom, "lat", [(i + 1, i) for i in range(count - 1)])
        north = jnp.where(northern, folded, above)
    return south, north, west, east


def partners(value, bits):
    axes = tuple(a for a in ("lon", "lat", "ens") if a in [b[0] for b in bits])
    flip = {a: 0 for a in axes}
    for a, b in bits:
        flip[a] ^= b
    return lax.ppermute(value, axes, route(axes, lambda *at: [i ^ flip[a] for a, i in zip(axes, at)]))


def summed(mine, other):
    axes = ("ens", "lon", "lat")
    bits = [(a, 1 << b) for a in axes for b in range(lax.axis_size(a).bit_length() - 1)]
    total = mine + partners(other, bits[:1]).astype(F32)
    rest = bits[2:4] + bits[1:2] + bits[4:] if lax.axis_size("lon") == 4 else bits[1:]
    while rest:
        pair, rest = rest[:2], rest[2:]
        sent = total.astype(BF16)
        if len(pair) == 2:
            far = partners(sent, pair)
            one, two = partners(sent, pair[:1]), partners(sent, pair[1:])
            total = (sent.astype(F32) + one.astype(F32)) + (two.astype(F32) + far.astype(F32))
        else:
            total = sent.astype(F32) + partners(sent, pair).astype(F32)
    return total, partners(total, bits[:1])


def fill(wide, south, block, north, west, east, sea=None):
    rows, cols = block.shape[0], block.shape[1]

    def inner(r, carry):
        value = block[r].astype(F32)
        if sea is not None:
            value = value * sea[r].astype(F32)
        wide[REACH + r, LEFT : LEFT + cols] = value
        wide[REACH + r, BASE:LEFT] = west[r].astype(F32)
        wide[REACH + r, LEFT + cols : LEFT + cols + REACH] = east[r].astype(F32)
        return carry

    lax.fori_loop(0, rows, inner, 0, unroll=2)

    def outer(r, carry):
        wide[r, BASE : LEFT + cols + REACH] = south[r].astype(F32)
        wide[REACH + rows + r, BASE : LEFT + cols + REACH] = north[r].astype(F32)
        return carry

    lax.fori_loop(0, REACH, outer, 0, unroll=2)


def conv(wide, tap, rows, cols, store):
    lines = rows // 2
    groups = math.gcd(cols // LANE, 4)

    def parity(q, carry):
        for first in range(0, cols // LANE, groups):
            sums = [[None] * groups for _ in range(lines)]
            for k in range(lines + KERNEL - 1):
                for j in range(KERNEL):
                    at = [BASE + (first + g) * LANE + DILATION * j for g in range(groups)]
                    values = [wide[q + 2 * k, a : a + LANE] for a in at]
                    for i in range(KERNEL):
                        line = k - i
                        if 0 <= line < lines:
                            weight = tap(k, i, j)
                            for g in range(groups):
                                term = weight * values[g]
                                old = sums[line][g]
                                sums[line][g] = term if old is None else old + term
            for line in range(lines):
                for g in range(groups):
                    store(q + 2 * line, (first + g) * LANE, sums[line][g])
        return carry

    lax.fori_loop(0, 2, parity, 0)


def forward_kernel(south, block, north, west, east, cotangent, sea, taps, gain, shift, up, down,
                   output, grad, parts, wide, mixed, spread):
    rows, cols, channels = block.shape
    hidden = up.shape[1]
    for k in range(TAPS):
        spread[k] = jnp.broadcast_to(taps[k : k + 1], (LANE, channels))
    fill(wide, south, block, north, west, east, sea)

    def store(row, col, value):
        mixed[row, col : col + LANE] = value

    conv(wide, lambda k, i, j: spread[i * KERNEL + j], rows, cols, store)

    up_w, down_w = up[...], down[...]
    gain_v, shift_v = gain[...], shift[...]
    lines = 4
    cells = lines * cols
    nt = (((1,), (1,)), ((), ()))
    tn = (((0,), (0,)), ((), ()))

    def chunk(n, carry):
        up_sum, down_sum, gain_sum, shift_sum = carry
        at = pl.ds(n * lines, lines)
        value = mixed[at].reshape(cells, channels)
        centered = value - jnp.mean(value, -1, keepdims=True)
        rstd = lax.rsqrt(jnp.mean(centered * centered, -1, keepdims=True) + 1e-06)
        unit = centered * rstd
        normed = (unit * gain_v + shift_v).astype(BF16)
        pre = jnp.dot(normed, up_w, preferred_element_type=F32)
        square = pre * pre
        tanh = jnp.tanh(pre * (SLOPE + (SLOPE * CUBIC) * square))
        gate = 0.5 + 0.5 * tanh
        activated = (pre * gate).astype(BF16)
        product = jnp.dot(activated, down_w, preferred_element_type=F32)
        ocean = sea[at].reshape(cells, channels).astype(F32)
        state = block[at].reshape(cells, channels).astype(F32)
        output[at] = ((state + product) * ocean).astype(BF16).reshape(lines, cols, channels)
        above = (cotangent[at] * sea[at]).reshape(cells, channels)
        down_sum = down_sum + lax.dot_general(above, activated, tn, preferred_element_type=F32)
        act_grad = lax.dot_general(above, down_w, nt, preferred_element_type=F32)
        deriv = gate + pre * (gate * (1.0 - tanh)) * (SLOPE + (3.0 * SLOPE * CUBIC) * square)
        pre_grad = (act_grad * deriv).astype(BF16)
        up_sum = up_sum + lax.dot_general(normed, pre_grad, tn, preferred_element_type=F32)
        norm_in = lax.dot_general(pre_grad, up_w, nt, preferred_element_type=F32)
        gain_sum = gain_sum + jnp.sum((norm_in * unit).reshape(cells // LANE, LANE, channels), 0)
        shift_sum = shift_sum + jnp.sum(norm_in.reshape(cells // LANE, LANE, channels), 0)
        scaled = norm_in * gain_v
        inner = jnp.mean(scaled * unit, -1, keepdims=True)
        result = rstd * (scaled - jnp.mean(scaled, -1, keepdims=True) - unit * inner)
        mixed[at] = result.reshape(lines, cols, channels)
        grad[at] = result.astype(BF16).reshape(lines, cols, channels)
        return up_sum, down_sum, gain_sum, shift_sum

    big = jnp.zeros((channels, hidden), F32)
    small = jnp.zeros((LANE, channels), F32)
    up_sum, down_sum, gain_sum, shift_sum = lax.fori_loop(
        0, rows // lines, chunk, (big, big, small, small)
    )
    parts[0:hidden] = down_sum.T
    for n in range(hidden // channels):
        start = hidden + n * channels
        parts[start : start + channels] = up_sum[:, n * channels : (n + 1) * channels]
    sums = [jnp.sum(gain_sum, 0, keepdims=True), jnp.sum(shift_sum, 0, keepdims=True)]
    parts[2 * hidden :] = jnp.concatenate(sums + [jnp.zeros((LANE - 2, channels), F32)], 0)


def kernel_kernel(odd, wide, mixed, parts, mine, other):
    rows, cols, channels = mixed.shape
    large = parts.shape[0] - LANE
    half = mine.shape[0]
    small = jnp.zeros((LANE, channels), F32)
    pieces = []
    for taps_i in (range(0, 4), range(4, KERNEL)):

        def quad(n, sums, taps_i=taps_i):
            base = (n // 2) * 8 + n % 2
            sums = list(sums)
            for g in range(cols // LANE):
                grads = [mixed[base + 2 * m, g * LANE : (g + 1) * LANE] for m in range(4)]
                for k in range(taps_i[0], taps_i[-1] + 4):
                    for j in range(KERNEL):
                        a = BASE + g * LANE + DILATION * j
                        value = wide[base + 2 * k, a : a + LANE]
                        for m in range(4):
                            if k - m in taps_i:
                                at = (k - m - taps_i[0]) * KERNEL + j
                                sums[at] = sums[at] + grads[m] * value
            return tuple(sums)

        zero = tuple(small for _ in range(len(taps_i) * KERNEL))
        pieces += list(lax.fori_loop(0, rows // 4, quad, zero))
    pieces = [jnp.sum(p, 0, keepdims=True) for p in pieces]
    pieces += [parts[large : large + 2], jnp.zeros((2 * half - large - TAPS - 2, channels), F32)]
    end = jnp.concatenate(pieces, 0)

    @pl.when(odd[0] == 0)
    def _():
        mine[...] = parts[0:half]
        other[0 : large - half] = parts[half:large].astype(BF16)
        other[large - half :] = end.astype(BF16)

    @pl.when(odd[0] != 0)
    def _():
        other[...] = parts[0:half].astype(BF16)
        mine[0 : large - half] = parts[half:large]
        mine[large - half :] = end


def final_kernel(odd, total, back, kernel_grad, norm_grad, up_grad, down_grad, whole, *, factor):
    half = total.shape[0]
    hidden, channels = down_grad.shape

    @pl.when(odd[0] == 0)
    def _():
        whole[0:half] = total[...] * factor
        whole[half:] = back[...] * factor

    @pl.when(odd[0] != 0)
    def _():
        whole[0:half] = back[...] * factor
        whole[half:] = total[...] * factor

    down_grad[...] = whole[0:hidden]
    for n in range(hidden // channels):
        start = hidden + n * channels
        up_grad[:, n * channels : (n + 1) * channels] = whole[start : start + channels]
    kernel_grad[...] = whole[2 * hidden : 2 * hidden + TAPS]
    norm_grad[...] = whole[2 * hidden + TAPS : 2 * hidden + TAPS + 2]


def backward_kernel(northern, south, block, north, west, east, cotangent, sea, taps,
                    field_grad, wide, spread, folded):
    rows, cols, channels = block.shape
    for k in range(TAPS):
        flipped = jnp.broadcast_to(taps[TAPS - 1 - k : TAPS - k], (LANE, channels))
        plain = jnp.broadcast_to(taps[k : k + 1], (LANE, channels))
        spread[k] = flipped
        folded[k] = jnp.where(northern[0] == 1, plain, flipped)
    fill(wide, south, block, north, west, east)
    edge = (REACH + rows) // 2

    def tap(k, i, j):
        return (folded if k >= edge else spread)[i * KERNEL + j]

    def store(row, col, value):
        at = (row, slice(col, col + LANE))
        field_grad[at] = ((cotangent[at].astype(F32) + value) * sea[at].astype(F32)).astype(BF16)

    conv(wide, tap, rows, cols, store)


def call(kernel, outs, operands, scratch=(), flags=0, work=0, name=None):
    vmem, smem = pl.BlockSpec(memory_space=pltpu.VMEM), pl.BlockSpec(memory_space=pltpu.SMEM)
    moved = sum(math.prod(a.shape) * a.dtype.itemsize for a in (*operands, *outs))
    return pl.pallas_call(
        kernel,
        out_shape=outs,
        in_specs=[smem] * flags + [vmem] * (len(operands) - flags),
        out_specs=[vmem] * len(outs),
        scratch_shapes=scratch,
        compiler_params=pltpu.CompilerParams(vmem_limit_bytes=24 * 1024 * 1024),
        cost_estimate=pl.CostEstimate(flops=work, bytes_accessed=moved, transcendentals=0),
        name=name,
    )(*operands)


def shards(field, cotangent, land_mask, kernel_taps, norm_gain, norm_shift, up_weight, down_weight):
    rows, cols, channels = field.shape[1:]
    hidden = up_weight.shape[1]
    shape = jax.ShapeDtypeStruct
    sea = jnp.broadcast_to(land_mask.astype(BF16)[:, :, None], (rows, cols, channels))
    state = field[0]
    south, north, west, east = extend(state * sea)
    tile = (rows, cols, channels)
    wide = (rows + 2 * REACH, cols + 2 * LEFT, channels)
    spread = pltpu.VMEM((TAPS, LANE, channels), F32)
    half = hidden + 32
    macs = TAPS * rows * cols * channels
    odd = (lax.axis_index("ens") % 2).astype(jnp.int32)[None]
    northern = is_northern().astype(jnp.int32)[None]
    output, grad, parts, widened, mixed_grad = call(
        forward_kernel,
        (shape(tile, BF16), shape(tile, BF16), shape((2 * hidden + LANE, channels), F32), shape(wide, F32), shape(tile, F32)),
        (south, state, north, west, east, cotangent[0], sea, kernel_taps, norm_gain[None], norm_shift[None], up_weight, down_weight),
        [spread],
        work=80 * macs,
        name="forward",
    )
    mine, other = call(
        kernel_kernel,
        (shape((half, channels), F32), shape((half, channels), BF16)),
        (odd, widened, mixed_grad, parts),
        flags=1,
        work=20 * macs,
        name="kernel_gradient",
    )
    south, north, west, east = extend(grad)
    (field_grad,) = call(
        backward_kernel,
        (shape(tile, BF16),),
        (northern, south, grad, north, west, east, cotangent[0], sea, kernel_taps),
        [pltpu.VMEM(wide, F32), spread, spread],
        flags=1,
        work=30 * macs,
        name="backward",
    )
    count = rows * cols * lax.axis_size("lon") * lax.axis_size("lat") * lax.axis_size("ens")
    total, back = summed(mine, other)
    kernel_grad, norm_grad, up_grad, down_grad = call(
        functools.partial(final_kernel, factor=1.0 / math.sqrt(count)),
        (shape((TAPS, channels), F32), shape((2, channels), F32), shape((channels, hidden), F32), shape((hidden, channels), F32)),
        (odd, total, back),
        [pltpu.VMEM((2 * half, channels), F32)],
        flags=1,
        name="final",
    )
    return output[None], field_grad[None], kernel_grad, norm_grad, up_grad, down_grad


def solution(mesh):
    grid = P("ens", "lat", "lon", None)
    return jax.shard_map(
        shards,
        mesh=mesh,
        in_specs=(grid, grid, P("lat", "lon"), P(), P(), P(), P(), P()),
        out_specs=(grid, grid, P(), P(), P(), P()),
        check_vma=False,
    )
```

```python
import functools
import math

import jax
import jax.numpy as jnp
from jax import lax
from jax.experimental import pallas as pl
from jax.experimental.pallas import tpu as pltpu
from jax.sharding import PartitionSpec as P

KERNEL = 7
DILATION = 2
REACH = 6
TAPS = KERNEL * KERNEL
LANE = 8
LEFT = 8
BASE = LEFT - REACH
SLOPE = math.sqrt(2.0 / math.pi)
CUBIC = 0.044715
F32, BF16 = jnp.float32, jnp.bfloat16


def route(axes, target):
    sizes = [lax.axis_size(a) for a in axes]
    pairs = []
    for flat in range(math.prod(sizes)):
        rest, at = flat, []
        for size in reversed(sizes):
            at.append(rest % size)
            rest //= size
        at = at[::-1]
        to = target(*at)
        if to is not None:
            dest = 0
            for size, i in zip(sizes, to):
                dest = dest * size + i
            pairs.append((flat, dest))
    return pairs


def is_northern():
    return lax.axis_index("lat") == lax.axis_size("lat") - 1


def xor_partner(value, axis, bits):
    return lax.ppermute(value, axis, [(i, i ^ bits) for i in range(lax.axis_size(axis))])


def across(block):
    lats, lons = lax.axis_size("lat"), lax.axis_size("lon")
    top, bottom, northern = block[block.shape[0] - REACH :], block[:REACH], is_northern()
    folded = lax.ppermute(top[::-1, ::-1], "lon", [(i, lons - 1 - i) for i in range(lons)])
    if lats == 2:
        facing = xor_partner(jnp.where(northern, bottom, top), "lat", 1)
        return facing, facing, folded
    below = lax.ppermute(top, "lat", [(i, i + 1) for i in range(lats - 1)])
    return below, lax.ppermute(bottom, "lat", [(i + 1, i) for i in range(lats - 1)]), folded


def sides_kernel(flags, below, above, folded, block, *refs):
    south, north, first, last = refs[-4:]
    rows, cols = block.shape[0], block.shape[1]
    northern, swap = flags[0] == 1, flags[1] == 1

    def put(row, value):
        head, tail = value[:REACH], value[cols - REACH :]
        first[row] = jnp.where(swap, tail, head).astype(BF16)
        last[row] = jnp.where(swap, head, tail).astype(BF16)

    for r in range(REACH):
        low = below[r].astype(F32)
        low = jnp.where(flags[2] == 1, low, 0.0)
        high = jnp.where(northern, folded[r].astype(F32), above[r].astype(F32))
        south[r], north[r] = low.astype(BF16), high.astype(BF16)
        put(r, low)
        put(REACH + rows + r, high)
    for r in range(rows):
        put(REACH + r, block[r].astype(F32))


def along(rows_in, block, *after):
    lons = lax.axis_size("lon")
    rows, cols, channels = block.shape
    pairs = lons == 4
    odd = lax.axis_index("lon") % 2 if pairs else 0
    flags = jnp.stack([is_northern().astype(jnp.int32), jnp.asarray(odd, jnp.int32), (lax.axis_index("lat") > 0).astype(jnp.int32)])
    shape = jax.ShapeDtypeStruct
    strip, side = shape((REACH, cols, channels), BF16), shape((rows + 2 * REACH, REACH, channels), BF16)
    south, north, first, last = call(
        sides_kernel, (strip, strip, side, side), (flags, *rows_in, block, *after), flags=1, name="sides"
    )
    if pairs:
        far, near = xor_partner(first, "lon", 3), xor_partner(last, "lon", 1)
        return south, north, jnp.where(odd == 0, far, near), jnp.where(odd == 0, near, far)
    ring = [(i, (i + 1) % lons) for i in range(lons)]
    west = lax.ppermute(last, "lon", ring)
    return south, north, west, lax.ppermute(first, "lon", [(j, i) for i, j in ring])


def partners(value, bits):
    axes = tuple(a for a in ("lon", "lat", "ens") if a in [b[0] for b in bits])
    flip = {a: 0 for a in axes}
    for a, b in bits:
        flip[a] ^= b
    return lax.ppermute(value, axes, route(axes, lambda *at: [i ^ flip[a] for a, i in zip(axes, at)]))


def add_kernel(*refs):
    refs[-1][...] = added([ref[...] for ref in refs[:-2]])


def stages():
    bits = {a: [(a, 1 << b) for b in range(lax.axis_size(a).bit_length() - 1)] for a in ("ens", "lat", "lon")}
    rest = bits["ens"][1:] + bits["lat"] + bits["lon"]
    return bits["ens"][:1], [rest[n : n + 2] for n in range(0, len(rest), 2)]


def stage(total, pair):
    sent = total.astype(BF16)
    if len(pair) == 1:
        return [sent, partners(sent, pair)]
    far = partners(sent, pair)
    return [sent, partners(sent, pair[:1]), partners(sent, pair[1:]), far]


def added(values):
    values = [v.astype(F32) for v in values]
    return sum(values) if len(values) == 2 else (values[0] + values[1]) + (values[2] + values[3])


def fill(wide, south, block, north, west, east):
    rows, cols = block.shape[0], block.shape[1]
    for ref, start, count in ((south, 0, REACH), (block, REACH, rows), (north, REACH + rows, REACH)):

        def one(r, carry, ref=ref, start=start):
            wide[start + r, LEFT : LEFT + cols] = ref[r].astype(F32)
            return carry

        lax.fori_loop(0, count, one, 0, unroll=2)

    def sides(r, carry):
        wide[r, BASE:LEFT] = west[r].astype(F32)
        wide[r, LEFT + cols : LEFT + cols + REACH] = east[r].astype(F32)
        return carry

    lax.fori_loop(0, rows + 2 * REACH, sides, 0, unroll=4)


def conv(wide, tap, rows, cols, store):
    lines = rows // 2
    groups = math.gcd(cols // LANE, 4)

    def parity(q, carry):
        for first in range(0, cols // LANE, groups):
            sums = [[None] * groups for _ in range(lines)]
            for k in range(lines + KERNEL - 1):
                for j in range(KERNEL):
                    at = [BASE + (first + g) * LANE + DILATION * j for g in range(groups)]
                    values = [wide[q + 2 * k, a : a + LANE] for a in at]
                    for i in range(KERNEL):
                        line = k - i
                        if 0 <= line < lines:
                            weight = tap(k, i, j)
                            for g in range(groups):
                                term = weight * values[g]
                                old = sums[line][g]
                                sums[line][g] = term if old is None else old + term
            for line in range(lines):
                for g in range(groups):
                    store(q + 2 * line, (first + g) * LANE, sums[line][g])
        return carry

    lax.fori_loop(0, 2, parity, 0)


def mask_kernel(field, mask, masked, sea, state, ocean, sems):
    rows, cols, channels = state.shape
    copies = [pltpu.make_async_copy(field, state, sems.at[0]), pltpu.make_async_copy(mask, ocean, sems.at[1])]
    for copy in copies:
        copy.start()
    copies[1].wait()
    value = ocean[...].astype(BF16)
    at = lax.broadcasted_iota(jnp.int32, (rows, channels), 0)
    for r in range(rows):
        pick = jnp.where(at == r, 1.0, 0.0).astype(BF16)
        row = lax.dot_general(value, pick, (((0,), (0,)), ((), ())), preferred_element_type=F32)
        sea[r] = row.astype(BF16)
    copies[0].wait()
    for r in range(rows):
        masked[r] = state[r] * sea[r]


def forward_kernel(south, block, north, west, east, cotangent, sea, taps, gain, shift, up, down,
                   output, grad, parts, wide, mixed, spread, upstream, result, sems):
    rows, cols, channels = block.shape
    hidden = up.shape[1]
    fetch = pltpu.make_async_copy(cotangent, upstream, sems.at[0])
    fetch.start()
    for k in range(TAPS):
        spread[k] = jnp.broadcast_to(taps[k : k + 1], (LANE, channels))
    fill(wide, south, block, north, west, east)

    def store(row, col, value):
        mixed[row, col : col + LANE] = value

    conv(wide, lambda k, i, j: spread[i * KERNEL + j], rows, cols, store)

    up_w, down_w = up[...], down[...]
    gain_v, shift_v = gain[...], shift[...]
    lines = 4
    cells = lines * cols
    nt = (((1,), (1,)), ((), ()))
    tn = (((0,), (0,)), ((), ()))

    def send(n):
        at = pl.ds(n * lines, lines)
        return pltpu.make_async_copy(result.at[at], output.at[at], sems.at[1 + n])

    def chunk(n, carry):
        up_sum, down_sum, gain_sum, shift_sum = carry
        at = pl.ds(n * lines, lines)
        value = mixed[at].reshape(cells, channels)
        centered = value - jnp.mean(value, -1, keepdims=True)
        rstd = lax.rsqrt(jnp.mean(centered * centered, -1, keepdims=True) + 1e-06)
        unit = centered * rstd
        normed = (unit * gain_v + shift_v).astype(BF16)
        pre = jnp.dot(normed, up_w, preferred_element_type=F32)
        square = pre * pre
        tanh = jnp.tanh(pre * (SLOPE + (SLOPE * CUBIC) * square))
        gate = 0.5 + 0.5 * tanh
        activated = (pre * gate).astype(BF16)
        product = jnp.dot(activated, down_w, preferred_element_type=F32)
        ocean = sea[at].reshape(cells, channels).astype(F32)
        state = block[at].reshape(cells, channels).astype(F32)
        result[at] = ((state + product) * ocean).astype(BF16).reshape(lines, cols, channels)
        send(n).start()
        above = (upstream[at] * sea[at]).reshape(cells, channels)
        down_sum = down_sum + lax.dot_general(above, activated, tn, preferred_element_type=F32)
        act_grad = lax.dot_general(above, down_w, nt, preferred_element_type=F32)
        deriv = gate + pre * (gate * (1.0 - tanh)) * (SLOPE + (3.0 * SLOPE * CUBIC) * square)
        pre_grad = (act_grad * deriv).astype(BF16)
        up_sum = up_sum + lax.dot_general(normed, pre_grad, tn, preferred_element_type=F32)
        norm_in = lax.dot_general(pre_grad, up_w, nt, preferred_element_type=F32)
        gain_sum = gain_sum + jnp.sum((norm_in * unit).reshape(cells // LANE, LANE, channels), 0)
        shift_sum = shift_sum + jnp.sum(norm_in.reshape(cells // LANE, LANE, channels), 0)
        scaled = norm_in * gain_v
        inner = jnp.mean(scaled * unit, -1, keepdims=True)
        moved = rstd * (scaled - jnp.mean(scaled, -1, keepdims=True) - unit * inner)
        mixed[at] = moved.reshape(lines, cols, channels)
        grad[at] = moved.astype(BF16).reshape(lines, cols, channels)
        return up_sum, down_sum, gain_sum, shift_sum

    big = jnp.zeros((channels, hidden), F32)
    small = jnp.zeros((LANE, channels), F32)
    fetch.wait()
    up_sum, down_sum, gain_sum, shift_sum = lax.fori_loop(
        0, rows // lines, chunk, (big, big, small, small)
    )
    parts[0:hidden] = down_sum.T
    for n in range(hidden // channels):
        start = hidden + n * channels
        parts[start : start + channels] = up_sum[:, n * channels : (n + 1) * channels]
    sums = [jnp.sum(gain_sum, 0, keepdims=True), jnp.sum(shift_sum, 0, keepdims=True)]
    parts[2 * hidden :] = jnp.concatenate(sums + [jnp.zeros((LANE - 2, channels), F32)], 0)
    for n in range(rows // lines):
        send(n).wait()


def kernel_kernel(odd, wide, mixed, parts, mine, other):
    rows, cols, channels = mixed.shape
    large = parts.shape[0] - LANE
    half = mine.shape[0]
    small = jnp.zeros((LANE, channels), F32)
    pieces = []
    for taps_i in (range(0, 4), range(4, KERNEL)):

        def quad(n, sums, taps_i=taps_i):
            base = (n // 2) * 8 + n % 2
            sums = list(sums)
            for g in range(cols // LANE):
                grads = [mixed[base + 2 * m, g * LANE : (g + 1) * LANE] for m in range(4)]
                for k in range(taps_i[0], taps_i[-1] + 4):
                    for j in range(KERNEL):
                        a = BASE + g * LANE + DILATION * j
                        value = wide[base + 2 * k, a : a + LANE]
                        for m in range(4):
                            if k - m in taps_i:
                                at = (k - m - taps_i[0]) * KERNEL + j
                                sums[at] = sums[at] + grads[m] * value
            return tuple(sums)

        zero = tuple(small for _ in range(len(taps_i) * KERNEL))
        pieces += list(lax.fori_loop(0, rows // 4, quad, zero))
    pieces = [jnp.sum(p, 0, keepdims=True) for p in pieces]
    pieces += [parts[large : large + 2], jnp.zeros((2 * half - large - TAPS - 2, channels), F32)]
    end = jnp.concatenate(pieces, 0)

    @pl.when(odd[0] == 0)
    def _():
        mine[...] = parts[0:half]
        other[0 : large - half] = parts[half:large].astype(BF16)
        other[large - half :] = end.astype(BF16)

    @pl.when(odd[0] != 0)
    def _():
        other[...] = parts[0:half].astype(BF16)
        mine[0 : large - half] = parts[half:large]
        mine[large - half :] = end


def final_kernel(odd, total, back, kernel_grad, norm_grad, up_grad, down_grad, whole, *, factor):
    half = total.shape[0]
    hidden, channels = down_grad.shape

    @pl.when(odd[0] == 0)
    def _():
        whole[0:half] = total[...] * factor
        whole[half:] = back[...] * factor

    @pl.when(odd[0] != 0)
    def _():
        whole[0:half] = back[...] * factor
        whole[half:] = total[...] * factor

    down_grad[...] = whole[0:hidden]
    for n in range(hidden // channels):
        start = hidden + n * channels
        up_grad[:, n * channels : (n + 1) * channels] = whole[start : start + channels]
    kernel_grad[...] = whole[2 * hidden : 2 * hidden + TAPS]
    norm_grad[...] = whole[2 * hidden + TAPS : 2 * hidden + TAPS + 2]


def backward_kernel(northern, south, block, north, west, east, cotangent, sea, taps,
                    field_grad, token, wide, spread, folded):
    rows, cols, channels = block.shape
    for k in range(TAPS):
        flipped = jnp.broadcast_to(taps[TAPS - 1 - k : TAPS - k], (LANE, channels))
        plain = jnp.broadcast_to(taps[k : k + 1], (LANE, channels))
        spread[k] = flipped
        folded[k] = jnp.where(northern[0] == 1, plain, flipped)
    fill(wide, south, block, north, west, east)
    edge = (REACH + rows) // 2

    def tap(k, i, j):
        return (folded if k >= edge else spread)[i * KERNEL + j]

    def store(row, col, value):
        at = (row, slice(col, col + LANE))
        field_grad[at] = ((cotangent[at].astype(F32) + value) * sea[at].astype(F32)).astype(BF16)

    conv(wide, tap, rows, cols, store)
    token[...] = jnp.zeros_like(token)


def call(kernel, outs, operands, scratch=(), flags=0, far=(), far_outs=(), work=0, name=None):
    vmem, smem = pl.BlockSpec(memory_space=pltpu.VMEM), pl.BlockSpec(memory_space=pltpu.SMEM)
    anywhere = pl.BlockSpec(memory_space=pl.ANY)
    moved = sum(math.prod(a.shape) * a.dtype.itemsize for a in (*operands, *outs))
    return pl.pallas_call(
        kernel,
        out_shape=outs,
        in_specs=[smem if n < flags else anywhere if n in far else vmem for n in range(len(operands))],
        out_specs=[anywhere if n in far_outs else vmem for n in range(len(outs))],
        scratch_shapes=scratch,
        compiler_params=pltpu.CompilerParams(vmem_limit_bytes=24 * 1024 * 1024),
        cost_estimate=pl.CostEstimate(flops=work, bytes_accessed=moved, transcendentals=0),
        name=name,
    )(*operands)


def shards(field, cotangent, land_mask, kernel_taps, norm_gain, norm_shift, up_weight, down_weight):
    rows, cols, channels = field.shape[1:]
    hidden = up_weight.shape[1]
    shape = jax.ShapeDtypeStruct
    tile = (rows, cols, channels)
    near = pltpu.VMEM(tile, BF16)
    state, sea = call(
        mask_kernel,
        (shape(tile, BF16), shape(tile, BF16)),
        (field[0], land_mask),
        [near, pltpu.VMEM((rows, cols), jnp.int32), pltpu.SemaphoreType.DMA((2,))],
        far=(0, 1),
        work=10**9,
        name="mask",
    )
    south, north, west, east = along(across(state), state)
    wide = (rows + 2 * REACH, cols + 2 * LEFT, channels)
    spread = pltpu.VMEM((TAPS, LANE, channels), F32)
    half = hidden + 32
    odd = (lax.axis_index("ens") % 2).astype(jnp.int32)[None]
    northern = is_northern().astype(jnp.int32)[None]
    output, grad, parts, widened, mixed_grad = call(
        forward_kernel,
        (shape(tile, BF16), shape(tile, BF16), shape((2 * hidden + LANE, channels), F32), shape(wide, F32), shape(tile, F32)),
        (south, state, north, west, east, cotangent[0], sea, kernel_taps, norm_gain[None], norm_shift[None], up_weight, down_weight),
        [spread, near, near, pltpu.SemaphoreType.DMA((1 + rows,))],
        far=(5,),
        far_outs=(0,),
        work=6 * 10**9,
        name="forward",
    )
    crossed = across(grad)
    mine, other = call(
        kernel_kernel,
        (shape((half, channels), F32), shape((half, channels), BF16)),
        (odd, widened, mixed_grad, parts),
        flags=1,
        work=2 * 10**9,
        name="kernel_gradient",
    )
    core, rest = stages()
    total = mine + partners(other, core).astype(F32)
    values = stage(total, rest[0])
    south, north, west, east = along(crossed, grad, values[-1])
    for pair in rest[1:]:
        values = stage(added(values), pair)
    field_grad, token = call(
        backward_kernel,
        (shape(tile, BF16), shape((LANE, channels), F32)),
        (northern, south, grad, north, west, east, cotangent[0], sea, kernel_taps),
        [pltpu.VMEM(wide, F32), spread, spread],
        flags=1,
        work=3 * 10**9,
        name="backward",
    )
    (total,) = call(add_kernel, (shape(mine.shape, F32),), (*values, token), name="add")
    back = partners(total, core)
    count = rows * cols * lax.axis_size("lon") * lax.axis_size("lat") * lax.axis_size("ens")
    kernel_grad, norm_grad, up_grad, down_grad = call(
        functools.partial(final_kernel, factor=1.0 / math.sqrt(count)),
        (shape((TAPS, channels), F32), shape((2, channels), F32), shape((channels, hidden), F32), shape((hidden, channels), F32)),
        (odd, total, back),
        [pltpu.VMEM((2 * half, channels), F32)],
        flags=1,
        name="final",
    )
    return output[None], field_grad[None], kernel_grad, norm_grad, up_grad, down_grad


def solution(mesh):
    grid = P("ens", "lat", "lon", None)
    return jax.shard_map(
        shards,
        mesh=mesh,
        in_specs=(grid, grid, P("lat", "lon"), P(), P(), P(), P(), P()),
        out_specs=(grid, grid, P(), P(), P(), P()),
        check_vma=False,
    )
```

```python
import functools
import math

import jax
import jax.numpy as jnp
from jax import lax
from jax.experimental import pallas as pl
from jax.experimental.pallas import tpu as pltpu
from jax.sharding import PartitionSpec as P

KERNEL = 7
DILATION = 2
REACH = 6
TAPS = KERNEL * KERNEL
LANE = 8
LEFT = 8
BASE = LEFT - REACH
LOWER_WORK, UPPER_WORK, KERNEL_WORK = 10**8, 2 * 10**9, 10**8
SLOPE = math.sqrt(2.0 / math.pi)
CUBIC = 0.044715
F32, BF16 = jnp.float32, jnp.bfloat16


def route(axes, target):
    sizes = [lax.axis_size(a) for a in axes]
    pairs = []
    for flat in range(math.prod(sizes)):
        rest, at = flat, []
        for size in reversed(sizes):
            at.append(rest % size)
            rest //= size
        at = at[::-1]
        to = target(*at)
        if to is not None:
            dest = 0
            for size, i in zip(sizes, to):
                dest = dest * size + i
            pairs.append((flat, dest))
    return pairs


def is_northern():
    return lax.axis_index("lat") == lax.axis_size("lat") - 1


def xor_partner(value, axis, bits):
    return lax.ppermute(value, axis, [(i, i ^ bits) for i in range(lax.axis_size(axis))])


NORTHERN, ODD, INNER, CORE = range(4)


def flags_of():
    odd = lax.axis_index("lon") % 2 if lax.axis_size("lon") == 4 else 0
    values = (is_northern(), odd, lax.axis_index("lat") > 0, lax.axis_index("ens") % 2)
    row = lax.broadcasted_iota(jnp.int32, (LANE, 128), 0)
    return sum(jnp.where(row == n, jnp.asarray(v, jnp.int32), 0) for n, v in enumerate(values))


def on(flags, n):
    return flags[n : n + 1] == 1


def rim_kernel(block, flags, facing, near, far):
    rows, cols = block.shape[0], block.shape[1]
    northern, odd = on(flags, NORTHERN), on(flags, ODD)
    for k in range(REACH):
        low, high = block[k].astype(F32), block[rows - REACH + k].astype(F32)
        facing[k] = jnp.where(northern, low, high).astype(BF16)
    for r in range(rows):
        head = block[r, : 2 * LANE].astype(F32)[:LANE]
        tail = block[r, cols - 2 * LANE :].astype(F32)[LANE:]
        near[r] = jnp.where(odd, head, tail).astype(BF16)
        far[r] = jnp.where(odd, tail, head).astype(BF16)


def fold_kernel(block, flags, far, *refs):
    joint, corner, own = refs[-3:]
    rows, cols, channels = block.shape
    start = 0
    odd = on(flags, ODD)
    down = lax.broadcasted_iota(jnp.int32, (cols, cols), 0)
    across = lax.broadcasted_iota(jnp.int32, (cols, cols), 1)
    turn = jnp.where(down + across == cols - 1, 1.0, 0.0).astype(BF16)
    if joint.shape[0] > REACH * cols:
        start = rows * LANE
        joint[:start] = far[...].astype(F32).reshape(start, channels).astype(BF16)
    for k in range(REACH):
        row = jnp.dot(turn, block[rows - 1 - k], preferred_element_type=F32)
        joint[start + k * cols : start + (k + 1) * cols] = row.astype(BF16)
        head, tail = row[:LANE], row[cols - LANE :]
        corner[k] = jnp.where(odd, tail, head).astype(BF16)
        own[k] = jnp.where(odd, head, tail).astype(BF16)


def put_corners(near, far, flags, facing, start=None):
    rows = near.shape[0]
    northern, odd = on(flags, NORTHERN), on(flags, ODD)
    for k in range(REACH):
        one, two = (
            jnp.where(northern, a[k].astype(F32), a[rows - REACH + k].astype(F32)) for a in (far, near)
        )
        sides = [jnp.where(odd, two, one), jnp.where(odd, one, two)]
        at = k if start is None else slice(start + k * 2 * LANE, start + (k + 1) * 2 * LANE)
        facing[at] = jnp.concatenate(sides, 0).astype(BF16)


def corner_kernel(near, far, flags, *refs):
    put_corners(near, far, flags, refs[-1])


def is_pairs():
    return (lax.axis_size("lat"), lax.axis_size("lon"), lax.axis_size("ens")) == (2, 4, 4)


def ring(axis, step, closed=True):
    count = lax.axis_size(axis)
    return [(i, (i + step) % count) for i in range(count) if closed or 0 <= i + step < count]


def extend_any(block):
    rows, cols, channels = block.shape
    lons = lax.axis_size("lon")
    top, bottom, flipped = block[rows - REACH :], block[:REACH], block[rows - REACH :][::-1, ::-1]
    west = lax.ppermute(block[:, cols - LANE :], "lon", ring("lon", 1))
    east = lax.ppermute(block[:, :LANE], "lon", ring("lon", -1))
    folded = lax.ppermute(flipped, "lon", [(i, lons - 1 - i) for i in range(lons)])
    left = lax.ppermute(folded[:, cols - LANE :], "lon", ring("lon", 1))
    right = lax.ppermute(folded[:, :LANE], "lon", ring("lon", -1))
    below = lax.ppermute(top, "lat", ring("lat", 1, False))
    above = lax.ppermute(bottom, "lat", ring("lat", -1, False))
    sides = [jnp.concatenate([west[at], east[at]], 1) for at in (slice(rows - REACH, rows), slice(REACH))]
    low = lax.ppermute(sides[0], "lat", ring("lat", 1, False))
    high = lax.ppermute(sides[1], "lat", ring("lat", -1, False))
    return below, above, folded, west, east, left, right, low, high


def shapes_of(block):
    rows, cols, channels = block.shape
    sizes = ((REACH, cols), (rows, LANE), (REACH, LANE), (REACH, 2 * LANE))
    return [jax.ShapeDtypeStruct((*size, channels), BF16) for size in sizes]


def extend(block, flags):
    if not is_pairs():
        return extend_any(block)
    strip, side, corner, corners = shapes_of(block)
    cells = side.shape[0] * side.shape[1]
    facing, near, far = call(rim_kernel, (strip, side, side), (block, flags), name="rim")
    facing, near = xor_partner(facing, "lat", 1), xor_partner(near, "lon", 1)
    both = jax.ShapeDtypeStruct((cells + strip.shape[0] * strip.shape[1], block.shape[2]), BF16)
    both, corner, own = call(fold_kernel, (both, corner, corner), (block, flags, far), name="fold")
    both, corner = xor_partner(both, "lon", 3), xor_partner(corner, "lon", 2)
    far, folded = both[:cells].reshape(side.shape), both[cells:].reshape(strip.shape)
    (corners,) = call(corner_kernel, (corners,), (near, far, flags, corner), name="corners")
    corners = xor_partner(corners, "lat", 1)
    return facing, facing, folded, far, near, own, corner, corners, corners


def partners(value, bits):
    axes = tuple(a for a in ("lon", "lat", "ens") if a in [b[0] for b in bits])
    flip = {a: 0 for a in axes}
    for a, b in bits:
        flip[a] ^= b
    return lax.ppermute(value, axes, route(axes, lambda *at: [i ^ flip[a] for a, i in zip(axes, at)]))


def add_kernel(*refs):
    rows, out = refs[-1].shape[0], refs[-1]
    out[...] = added([ref[:rows] for ref in refs[:-2]]).astype(out.dtype)


def stages():
    bits = {a: [(a, 1 << b) for b in range(lax.axis_size(a).bit_length() - 1)] for a in ("ens", "lat", "lon")}
    rest = bits["ens"][1:] + bits["lat"] + bits["lon"]
    return bits["ens"][:1], [rest[n : n + 2] for n in range(0, len(rest), 2)]


def stage(sent, pair):
    if len(pair) == 1:
        return [sent, partners(sent, pair)]
    far = partners(sent, pair)
    return [sent, partners(sent, pair[:1]), partners(sent, pair[1:]), far]


def added(values):
    values = [v.astype(F32) for v in values]
    return sum(values) if len(values) == 2 else (values[0] + values[1]) + (values[2] + values[3])


def add_kernel(*refs):
    rows, out = refs[-1].shape[0], refs[-1]
    out[...] = added([ref[:rows] for ref in refs[:-2]]).astype(out.dtype)


def join_corners_kernel(mine, core, small, near, far, flags, token, joined, wider):
    join_kernel(mine, core, small, joined)
    rows = joined.shape[0]
    wider[:rows] = joined[...]
    put_corners(near, far, flags, wider, rows)


def join_kernel(mine, core, small, *refs):
    (joined,) = refs[-1:]
    half = mine.shape[0]
    joined[:half] = (mine[...] + core[...].astype(F32)).astype(BF16)
    joined[half:] = small[...].astype(BF16)


def fill_own(wide, flags, block, below):
    rows, cols = block.shape[0], block.shape[1]
    inner = on(flags, INNER)
    for r in range(rows):
        wide[REACH + r, LEFT : LEFT + cols] = block[r].astype(F32)
    for k in range(REACH):
        wide[k, LEFT : LEFT + cols] = jnp.where(inner, below[k].astype(F32), 0.0)


def fill_top(wide, flags, above, folded):
    cols = above.shape[1]
    northern = on(flags, NORTHERN)
    for k in range(REACH):
        value = jnp.where(northern, folded[k].astype(F32), above[k].astype(F32))
        wide[wide.shape[0] - REACH + k, LEFT : LEFT + cols] = value


def fill_sides(wide, flags, far, near, own, corner, low, high):
    rows, right = far.shape[0], wide.shape[1] - LEFT
    northern, odd, inner = on(flags, NORTHERN), on(flags, ODD), on(flags, INNER)
    for r in range(rows):
        one, two = far[r].astype(F32), near[r].astype(F32)
        wide[REACH + r, :LEFT] = jnp.where(odd, two, one)
        wide[REACH + r, right:] = jnp.where(odd, one, two)
    for k in range(REACH):
        sides = jnp.where(inner, low[k].astype(F32), 0.0)
        wide[k, :LEFT], wide[k, right:] = sides[:LANE], sides[LANE:]
        sides, one, two = high[k].astype(F32), own[k].astype(F32), corner[k].astype(F32)
        top = REACH + rows + k
        wide[top, :LEFT] = jnp.where(northern, jnp.where(odd, two, one), sides[:LANE])
        wide[top, right:] = jnp.where(northern, jnp.where(odd, one, two), sides[LANE:])


def conv(wide, tap, first, rows, starts, store):
    lines = rows // 2
    chunk = max(1, 32 // lines)

    def parity(q, carry):
        for n in range(0, len(starts), chunk):
            cols = starts[n : n + chunk]
            sums = [[None] * len(cols) for _ in range(lines)]
            for k in range(lines + KERNEL - 1):
                for j in range(KERNEL):
                    at = [BASE + c + DILATION * j for c in cols]
                    values = [wide[first + q + 2 * k, a : a + LANE] for a in at]
                    for i in range(KERNEL):
                        line = k - i
                        if 0 <= line < lines:
                            weight = tap(k, i, j)
                            for g, value in enumerate(values):
                                term, old = weight * value, sums[line][g]
                                sums[line][g] = term if old is None else old + term
            for line in range(lines):
                for g, c in enumerate(cols):
                    store(first + q + 2 * line, c, sums[line][g])
        return carry

    lax.fori_loop(0, 2, parity, 0)


def mask_kernel(field, mask, masked, sea, state, ocean, sems):
    rows, cols, channels = state.shape
    copies = [pltpu.make_async_copy(field, state, sems.at[0]), pltpu.make_async_copy(mask, ocean, sems.at[1])]
    for copy in copies:
        copy.start()
    copies[1].wait()
    value = ocean[...].astype(BF16)
    at = lax.broadcasted_iota(jnp.int32, (rows, channels), 0)
    for r in range(rows):
        pick = jnp.where(at == r, 1.0, 0.0).astype(BF16)
        row = lax.dot_general(value, pick, (((0,), (0,)), ((), ())), preferred_element_type=F32)
        sea[r] = row.astype(BF16)
    copies[0].wait()
    for r in range(rows):
        masked[r] = state[r] * sea[r]


def block_pass(first, rows, blocks, spread, sea, weights, state, arrive=None):
    wide, mixed, result, grad, upstream, up_part, down_part, sums = state
    taps, gain, shift, up, down = weights
    channels = wide.shape[2]
    for k in range(TAPS):
        spread[k] = jnp.broadcast_to(taps[k : k + 1], (LANE, channels))

    def store(row, col, value):
        mixed[row, col : col + LANE] = value

    starts = [c for col, cols in blocks for c in range(col, col + cols, LANE)]
    conv(wide, lambda k, i, j: spread[i * KERNEL + j], first, rows, starts, store)
    width = sum(cols for _, cols in blocks)
    cells = rows * width

    def take(ref, row=0, col=0):
        parts = [ref[first + row : first + row + rows, col + c : col + c + n].astype(F32) for c, n in blocks]
        return jnp.concatenate(parts, 1).reshape(cells, channels)

    def put(ref, value):
        value, at = value.reshape(rows, width, channels), 0
        for c, n in blocks:
            ref[first : first + rows, c : c + n] = value[:, at : at + n].astype(ref.dtype)
            at += n

    up_w, down_w, gain_v = up[...], down[...], gain[...]
    nt = (((1,), (1,)), ((), ()))
    tn = (((0,), (0,)), ((), ()))
    value = take(mixed)
    centered = value - jnp.mean(value, -1, keepdims=True)
    rstd = lax.rsqrt(jnp.mean(centered * centered, -1, keepdims=True) + 1e-06)
    unit = centered * rstd
    normed = (unit * gain_v + shift[...]).astype(BF16)
    pre = jnp.dot(normed, up_w, preferred_element_type=F32)
    square = pre * pre
    tanh = jnp.tanh(pre * (SLOPE + (SLOPE * CUBIC) * square))
    gate = 0.5 + 0.5 * tanh
    activated = (pre * gate).astype(BF16)
    product = jnp.dot(activated, down_w, preferred_element_type=F32)
    ocean = take(sea)
    put(result, (take(wide, REACH, LEFT) + product) * ocean)
    if arrive is not None:
        arrive()
    above = (take(upstream) * ocean).astype(BF16)
    down_part[...] += lax.dot_general(above, activated, tn, preferred_element_type=F32)
    act_grad = lax.dot_general(above, down_w, nt, preferred_element_type=F32)
    deriv = gate + pre * (gate * (1.0 - tanh)) * (SLOPE + (3.0 * SLOPE * CUBIC) * square)
    pre_grad = (act_grad * deriv).astype(BF16)
    up_part[...] += lax.dot_general(normed, pre_grad, tn, preferred_element_type=F32)
    norm_in = lax.dot_general(pre_grad, up_w, nt, preferred_element_type=F32)
    sums[0] += jnp.sum((norm_in * unit).reshape(cells // LANE, LANE, channels), 0)
    sums[1] += jnp.sum(norm_in.reshape(cells // LANE, LANE, channels), 0)
    scaled = norm_in * gain_v
    inner = jnp.mean(scaled * unit, -1, keepdims=True)
    moved = rstd * (scaled - jnp.mean(scaled, -1, keepdims=True) - unit * inner)
    put(mixed, moved)
    put(grad, moved)


STATE = 8


def lower_kernel(block, below, cotangent, sea, flags, *refs):
    weights, state, (spread, sem) = refs[:5], refs[5:-2], refs[-2:]
    rows, cols = block.shape[0], block.shape[1]
    upstream, up_part, down_part, sums = state[4:]
    fetch = pltpu.make_async_copy(cotangent, upstream, sem)
    fetch.start()
    for ref in (up_part, down_part, sums):
        ref[...] = jnp.zeros_like(ref)
    fill_own(state[0], flags, block, below)
    block_pass(0, rows // 2, [(LANE, cols - 2 * LANE)], spread, sea, weights, state, fetch.wait)


def upper_kernel(*refs):
    above, folded, sea, flags = refs[STATE : STATE + 4]
    weights, state, spread = refs[STATE + 4 : STATE + 9], refs[STATE + 9 : -1], refs[-1]
    rows, cols = sea.shape[0], sea.shape[1]
    fill_top(state[0], flags, above, folded)
    block_pass(rows // 2, rows // 2, [(LANE, cols - 2 * LANE)], spread, sea, weights, state)


def edge_kernel(*refs):
    sides, sea, flags = refs[STATE : STATE + 6], refs[STATE + 6], refs[STATE + 7]
    weights, state, (mine, other, spread) = refs[STATE + 8 : STATE + 13], refs[STATE + 13 : -3], refs[-3:]
    rows, cols = sea.shape[0], sea.shape[1]
    hidden, channels = mine.shape
    fill_sides(state[0], flags, *sides)
    block_pass(0, rows, [(0, LANE), (cols - LANE, LANE)], spread, sea, weights, state)
    up_part, down_part = state[5:7]
    down_sum = down_part[...].T
    up_sum = jnp.concatenate([up_part[:, n : n + channels] for n in range(0, hidden, channels)], 0)
    odd = on(flags, CORE)
    mine[...] = jnp.where(odd, up_sum, down_sum)
    other[...] = jnp.where(odd, down_sum, up_sum).astype(BF16)


def kernel_kernel(wide, mixed, result, norm, output, small_out, sem):
    rows, cols, channels = mixed.shape
    send = pltpu.make_async_copy(result, output, sem)
    send.start()
    small = jnp.zeros((LANE, channels), F32)
    pieces = []
    for taps_i in (range(0, 4), range(4, KERNEL)):

        def quad(n, sums, taps_i=taps_i):
            base = (n // 2) * 8 + n % 2
            sums = list(sums)
            for g in range(cols // LANE):
                grads = [mixed[base + 2 * m, g * LANE : (g + 1) * LANE] for m in range(4)]
                for k in range(taps_i[0], taps_i[-1] + 4):
                    for j in range(KERNEL):
                        a = BASE + g * LANE + DILATION * j
                        value = wide[base + 2 * k, a : a + LANE]
                        for m in range(4):
                            if k - m in taps_i:
                                at = (k - m - taps_i[0]) * KERNEL + j
                                sums[at] = sums[at] + grads[m] * value
            return tuple(sums)

        zero = tuple(small for _ in range(len(taps_i) * KERNEL))
        pieces += list(lax.fori_loop(0, rows // 4, quad, zero))
    pieces += [norm[0], norm[1]]
    pieces = [jnp.sum(p, 0, keepdims=True) for p in pieces]
    pieces += [jnp.zeros((small_out.shape[0] - TAPS - 2, channels), F32)]
    small_out[...] = jnp.concatenate(pieces, 0)
    send.wait()


def final_kernel(total, back, flags, kernel_grad, norm_grad, up_grad, down_grad, *, factor):
    hidden, channels = down_grad.shape
    odd = on(flags, CORE)
    own, theirs = total[:hidden] * factor, back[:hidden] * factor
    down_grad[...] = jnp.where(odd, theirs, own)
    up = jnp.where(odd, own, theirs)
    for n in range(hidden // channels):
        up_grad[:, n * channels : (n + 1) * channels] = up[n * channels : (n + 1) * channels]
    small = (total[hidden:] + back[hidden:]) * factor
    kernel_grad[...] = small[:TAPS]
    norm_grad[...] = small[TAPS : TAPS + 2]


def backward_kernel(block, below, above, folded, far, near, own, corner, low, high, cotangent, sea, taps, flags,
                    field_grad, token, wide, spread, upper):
    rows, cols, channels = block.shape
    northern = on(flags, NORTHERN)
    for k in range(TAPS):
        flipped = jnp.broadcast_to(taps[TAPS - 1 - k : TAPS - k], (LANE, channels))
        plain = jnp.broadcast_to(taps[k : k + 1], (LANE, channels))
        spread[k] = flipped
        upper[k] = jnp.where(northern, plain, flipped)
    fill_own(wide, flags, block, below)
    fill_top(wide, flags, above, folded)
    fill_sides(wide, flags, far, near, own, corner, low, high)
    edge = (REACH + rows) // 2

    def tap(k, i, j):
        return (upper if k >= edge else spread)[i * KERNEL + j]

    def store(row, col, value):
        at = (row, slice(col, col + LANE))
        field_grad[at] = ((cotangent[at].astype(F32) + value) * sea[at].astype(F32)).astype(BF16)

    conv(wide, tap, 0, rows, list(range(0, cols, LANE)), store)
    token[...] = jnp.zeros_like(token)


def call(kernel, outs, operands, scratch=(), far=(), far_outs=(), aliases=(), work=0, name=None):
    vmem, hbm = pl.BlockSpec(memory_space=pltpu.VMEM), pl.BlockSpec(memory_space=pltpu.HBM)
    moved = sum(math.prod(a.shape) * a.dtype.itemsize for a in (*operands, *outs))
    return pl.pallas_call(
        kernel,
        out_shape=outs,
        in_specs=[hbm if n in far else vmem for n in range(len(operands))],
        out_specs=[hbm if n in far_outs else vmem for n in range(len(outs))],
        scratch_shapes=scratch,
        input_output_aliases=dict(aliases),
        compiler_params=pltpu.CompilerParams(vmem_limit_bytes=24 * 1024 * 1024),
        cost_estimate=pl.CostEstimate(flops=work, bytes_accessed=moved, transcendentals=0),
        name=name,
    )(*operands)


def shards(field, cotangent, land_mask, kernel_taps, norm_gain, norm_shift, up_weight, down_weight):
    rows, cols, channels = field.shape[1:]
    hidden = up_weight.shape[1]
    shape = jax.ShapeDtypeStruct
    tile = (rows, cols, channels)
    near = pltpu.VMEM(tile, BF16)
    masked, sea = call(
        mask_kernel,
        (shape(tile, BF16), shape(tile, BF16)),
        (field[0], land_mask),
        [near, pltpu.VMEM((rows, cols), jnp.int32), pltpu.SemaphoreType.DMA((2,))],
        far=(0, 1),
        work=10**9,
        name="mask",
    )
    flags = flags_of()
    below, above, folded, far, near, own, corner, low, high = extend(masked, flags)
    wide = (rows + 2 * REACH, cols + 2 * LEFT, channels)
    spread = pltpu.VMEM((TAPS, LANE, channels), F32)
    large, small = (hidden, channels), (64, channels)
    weights = (kernel_taps, norm_gain[None], norm_shift[None], up_weight, down_weight)
    part = shape((channels, hidden), F32)
    state = (shape(wide, F32), shape(tile, F32), shape(tile, BF16), shape(tile, BF16), shape(tile, BF16), part, part, shape((2, LANE, channels), F32))
    same = tuple((n, n) for n in range(STATE))
    passed = call(
        lower_kernel,
        state,
        (masked, below, cotangent[0], sea, flags, *weights),
        [spread, pltpu.SemaphoreType.DMA],
        far=(2,),
        work=LOWER_WORK,
        name="lower",
    )
    passed = call(upper_kernel, state, (*passed, above, folded, sea, flags, *weights), [spread], aliases=same, work=UPPER_WORK, name="upper")
    *passed, mine, other = call(
        edge_kernel,
        (*state, shape(large, F32), shape(large, BF16)),
        (*passed, far, near, own, corner, low, high, sea, flags, *weights),
        [spread],
        aliases=same,
        work=10**9,
        name="edge",
    )
    widened, mixed_grad, result, grad, upstream, _, _, sums = passed
    core, rest = stages()
    received = partners(other, core)
    output, last_sums = call(
        kernel_kernel,
        (shape(tile, BF16), shape(small, F32)),
        (widened, mixed_grad, result, sums),
        [pltpu.SemaphoreType.DMA],
        far_outs=(0,),
        work=KERNEL_WORK,
        name="kernel_gradient",
    )
    joined = shape((hidden + small[0], channels), BF16)
    if is_pairs():
        strip, side, corner, corners = shapes_of(grad)
        facing, near, far = call(rim_kernel, (strip, side, side), (grad, flags), name="rim")
        far_sent = far
        facing, near, far = xor_partner(facing, "lat", 1), xor_partner(near, "lon", 1), xor_partner(far, "lon", 3)
        folded, corner, own = call(
            fold_kernel,
            (shape((strip.shape[0] * strip.shape[1], channels), BF16), corner, corner),
            (grad, flags, far_sent, facing, received, last_sums),
            name="fold",
        )
        folded, corner = xor_partner(folded, "lon", 3), xor_partner(corner, "lon", 2)
        wider = shape((joined.shape[0] + corners.shape[0] * corners.shape[1], channels), BF16)
        sent, wider = call(
            join_corners_kernel, (joined, wider), (mine, received, last_sums, near, far, flags, own), name="join"
        )
        (one, two), cells = rest[0], joined.shape[0]
        wider = partners(wider, [two])
        values = [sent, partners(sent, [one]), wider, partners(sent, [one, two])]
        corners = wider[cells:].reshape(corners.shape)
        halo = (facing, facing, folded.reshape(strip.shape), far, near, own, corner, corners, corners)
    else:
        (sent,) = call(join_kernel, (joined,), (mine, received, last_sums), name="join")
        values = stage(sent, rest[0])
        halo = extend(grad, flags)
    for pair in rest[1:]:
        (sent,) = call(add_kernel, (shape(sent.shape, BF16),), (*values, halo[2]), name="add")
        values = stage(sent, pair)
    field_grad, token = call(
        backward_kernel,
        (shape(tile, BF16), shape((LANE, channels), F32)),
        (grad, *halo, upstream, sea, kernel_taps, flags),
        [pltpu.VMEM(wide, F32), spread, spread],
        work=3 * 10**9,
        name="backward",
    )
    (total,) = call(add_kernel, (shape(joined.shape, F32),), (*values, token), name="add")
    back = partners(total, core)
    count = rows * cols * lax.axis_size("lon") * lax.axis_size("lat") * lax.axis_size("ens")
    kernel_grad, norm_grad, up_grad, down_grad = call(
        functools.partial(final_kernel, factor=1.0 / math.sqrt(count)),
        (shape((TAPS, channels), F32), shape((2, channels), F32), shape((channels, hidden), F32), shape((hidden, channels), F32)),
        (total, back, flags),
        name="final",
    )
    return output[None], field_grad[None], kernel_grad, norm_grad, up_grad, down_grad


def solution(mesh):
    grid = P("ens", "lat", "lon", None)
    return jax.shard_map(
        shards,
        mesh=mesh,
        in_specs=(grid, grid, P("lat", "lon"), P(), P(), P(), P(), P()),
        out_specs=(grid, grid, P(), P(), P(), P()),
        check_vma=False,
    )
```

```python
import functools
import math

import jax
import jax.numpy as jnp
from jax import lax
from jax.experimental import pallas as pl
from jax.experimental.pallas import tpu as pltpu
from jax.sharding import PartitionSpec as P

KERNEL = 7
DILATION = 2
REACH = 6
TAPS = KERNEL * KERNEL
LANE = 8
LEFT = 8
BASE = LEFT - REACH
LOWER_WORK, UPPER_WORK, KERNEL_WORK = 10**8, 2 * 10**9, 10**8
SLOPE = math.sqrt(2.0 / math.pi)
CUBIC = 0.044715
F32, BF16 = jnp.float32, jnp.bfloat16


def route(axes, target):
    sizes = [lax.axis_size(a) for a in axes]
    pairs = []
    for flat in range(math.prod(sizes)):
        rest, at = flat, []
        for size in reversed(sizes):
            at.append(rest % size)
            rest //= size
        at = at[::-1]
        to = target(*at)
        if to is not None:
            dest = 0
            for size, i in zip(sizes, to):
                dest = dest * size + i
            pairs.append((flat, dest))
    return pairs


def is_northern():
    return lax.axis_index("lat") == lax.axis_size("lat") - 1


def xor_partner(value, axis, bits):
    return lax.ppermute(value, axis, [(i, i ^ bits) for i in range(lax.axis_size(axis))])


JOIN_TOKEN = 3
NORTHERN, ODD, INNER, CORE = range(4)


def flags_of():
    odd = lax.axis_index("lon") % 2 if lax.axis_size("lon") == 4 else 0
    values = (is_northern(), odd, lax.axis_index("lat") > 0, lax.axis_index("ens") % 2)
    row = lax.broadcasted_iota(jnp.int32, (LANE, 128), 0)
    return sum(jnp.where(row == n, jnp.asarray(v, jnp.int32), 0) for n, v in enumerate(values))


def on(flags, n):
    return flags[n : n + 1] == 1


def rim_kernel(block, flags, facing, near, far):
    rows, cols = block.shape[0], block.shape[1]
    northern, odd = on(flags, NORTHERN), on(flags, ODD)
    for k in range(REACH):
        low, high = block[k].astype(F32), block[rows - REACH + k].astype(F32)
        facing[k] = jnp.where(northern, low, high).astype(BF16)
    for r in range(rows):
        head = block[r, : 2 * LANE].astype(F32)[:LANE]
        tail = block[r, cols - 2 * LANE :].astype(F32)[LANE:]
        near[r] = jnp.where(odd, head, tail).astype(BF16)
        far[r] = jnp.where(odd, tail, head).astype(BF16)


def fold_kernel(block, flags, far, *refs):
    joint, corner, own = refs[-3:]
    rows, cols, channels = block.shape
    start = rows * LANE
    odd = on(flags, ODD)
    down = lax.broadcasted_iota(jnp.int32, (cols, cols), 0)
    across = lax.broadcasted_iota(jnp.int32, (cols, cols), 1)
    turn = jnp.where(down + across == cols - 1, 1.0, 0.0).astype(BF16)
    joint[:start] = far[...].astype(F32).reshape(start, channels).astype(BF16)
    for k in range(REACH):
        row = jnp.dot(turn, block[rows - 1 - k], preferred_element_type=F32)
        joint[start + k * cols : start + (k + 1) * cols] = row.astype(BF16)
        head, tail = row[:LANE], row[cols - LANE :]
        corner[k] = jnp.where(odd, tail, head).astype(BF16)
        own[k] = jnp.where(odd, head, tail).astype(BF16)


def corner_kernel(near, far, flags, *refs):
    (facing,) = refs[-1:]
    rows = near.shape[0]
    northern, odd = on(flags, NORTHERN), on(flags, ODD)
    for k in range(REACH):
        one, two = (
            jnp.where(northern, a[k].astype(F32), a[rows - REACH + k].astype(F32)) for a in (far, near)
        )
        sides = [jnp.where(odd, two, one), jnp.where(odd, one, two)]
        facing[k] = jnp.concatenate(sides, 0).astype(BF16)


def is_pairs():
    return (lax.axis_size("lat"), lax.axis_size("lon"), lax.axis_size("ens")) == (2, 4, 4)


def ring(axis, step, closed=True):
    count = lax.axis_size(axis)
    return [(i, (i + step) % count) for i in range(count) if closed or 0 <= i + step < count]


def extend_any(block):
    rows, cols, channels = block.shape
    lons = lax.axis_size("lon")
    top, bottom, flipped = block[rows - REACH :], block[:REACH], block[rows - REACH :][::-1, ::-1]
    west = lax.ppermute(block[:, cols - LANE :], "lon", ring("lon", 1))
    east = lax.ppermute(block[:, :LANE], "lon", ring("lon", -1))
    folded = lax.ppermute(flipped, "lon", [(i, lons - 1 - i) for i in range(lons)])
    left = lax.ppermute(folded[:, cols - LANE :], "lon", ring("lon", 1))
    right = lax.ppermute(folded[:, :LANE], "lon", ring("lon", -1))
    below = lax.ppermute(top, "lat", ring("lat", 1, False))
    above = lax.ppermute(bottom, "lat", ring("lat", -1, False))
    sides = [jnp.concatenate([west[at], east[at]], 1) for at in (slice(rows - REACH, rows), slice(REACH))]
    low = lax.ppermute(sides[0], "lat", ring("lat", 1, False))
    high = lax.ppermute(sides[1], "lat", ring("lat", -1, False))
    return below, above, folded, west, east, left, right, low, high


def shapes_of(block):
    rows, cols, channels = block.shape
    sizes = ((REACH, cols), (rows, LANE), (REACH, LANE), (REACH, 2 * LANE))
    return [jax.ShapeDtypeStruct((*size, channels), BF16) for size in sizes]


def extend(field, sea, flags):
    tile = jax.ShapeDtypeStruct(field.shape, BF16)
    if not is_pairs():
        (block,) = call(mask_kernel, (tile,), (field, sea), name="mask")
        return block, *extend_any(block)
    block, *pieces = round_one(mask_rim_kernel, (field, sea, flags), field, (tile,))
    return block, *round_two(pieces, flags, pieces[4])


def round_one(kernel, operands, block, outs=()):
    strip, side, corner, _ = shapes_of(block)
    both = jax.ShapeDtypeStruct((side.shape[0] * LANE + REACH * strip.shape[1], block.shape[2]), BF16)
    *made, facing, near, both, corner, own = call(
        kernel, (*outs, strip, side, both, corner, corner), operands, [pltpu.VMEM(side.shape, BF16)], work=2 * 10**9, name="rim"
    )
    both, facing = xor_partner(both, "lon", 3), xor_partner(facing, "lat", 1)
    near, corner = xor_partner(near, "lon", 1), xor_partner(corner, "lon", 2)
    return *made, facing, near, both, own, corner


def round_two(pieces, flags, *after):
    facing, near, both, own, corner = pieces
    rows, channels = near.shape[0], near.shape[2]
    cells = rows * LANE
    far, folded = both[:cells].reshape(near.shape), both[cells:].reshape(facing.shape)
    corners = jax.ShapeDtypeStruct((REACH, 2 * LANE, channels), BF16)
    (corners,) = call(corner_kernel, (corners,), (near, far, flags, *after), name="corners")
    corners = xor_partner(corners, "lat", 1)
    return facing, facing, folded, far, near, own, corner, corners, corners


def partners(value, bits):
    axes = tuple(a for a in ("lon", "lat", "ens") if a in [b[0] for b in bits])
    flip = {a: 0 for a in axes}
    for a, b in bits:
        flip[a] ^= b
    return lax.ppermute(value, axes, route(axes, lambda *at: [i ^ flip[a] for a, i in zip(axes, at)]))


def add_kernel(*refs):
    rows, out = refs[-1].shape[0], refs[-1]
    out[...] = added([ref[:rows] for ref in refs[:-2]]).astype(out.dtype)


def stages():
    bits = {a: [(a, 1 << b) for b in range(lax.axis_size(a).bit_length() - 1)] for a in ("ens", "lat", "lon")}
    rest = bits["ens"][1:] + bits["lat"] + bits["lon"]
    return bits["ens"][:1], [rest[n : n + 2] for n in range(0, len(rest), 2)]


def stage(sent, pair):
    if len(pair) == 1:
        return [sent, partners(sent, pair)]
    far = partners(sent, pair)
    return [sent, partners(sent, pair[:1]), partners(sent, pair[1:]), far]


def added(values):
    values = [v.astype(F32) for v in values]
    return sum(values) if len(values) == 2 else (values[0] + values[1]) + (values[2] + values[3])


def add_kernel(*refs):
    rows, out = refs[-1].shape[0], refs[-1]
    out[...] = added([ref[:rows] for ref in refs[:-2]]).astype(out.dtype)


def join_kernel(mine, core, small, *refs):
    (joined,) = refs[-1:]
    half = mine.shape[0]
    joined[:half] = (mine[...] + core[...].astype(F32)).astype(BF16)
    joined[half:] = small[...].astype(BF16)


def fill_own(wide, flags, block, below):
    rows, cols = block.shape[0], block.shape[1]
    inner = on(flags, INNER)
    for r in range(rows):
        wide[REACH + r, LEFT : LEFT + cols] = block[r].astype(F32)
    for k in range(REACH):
        wide[k, LEFT : LEFT + cols] = jnp.where(inner, below[k].astype(F32), 0.0)


def fill_top(wide, flags, above, folded):
    cols = above.shape[1]
    northern = on(flags, NORTHERN)
    for k in range(REACH):
        value = jnp.where(northern, folded[k].astype(F32), above[k].astype(F32))
        wide[wide.shape[0] - REACH + k, LEFT : LEFT + cols] = value


def fill_sides(wide, flags, far, near, own, corner, low, high):
    rows, right = far.shape[0], wide.shape[1] - LEFT
    northern, odd, inner = on(flags, NORTHERN), on(flags, ODD), on(flags, INNER)
    for r in range(rows):
        one, two = far[r].astype(F32), near[r].astype(F32)
        wide[REACH + r, :LEFT] = jnp.where(odd, two, one)
        wide[REACH + r, right:] = jnp.where(odd, one, two)
    for k in range(REACH):
        sides = jnp.where(inner, low[k].astype(F32), 0.0)
        wide[k, :LEFT], wide[k, right:] = sides[:LANE], sides[LANE:]
        sides, one, two = high[k].astype(F32), own[k].astype(F32), corner[k].astype(F32)
        top = REACH + rows + k
        wide[top, :LEFT] = jnp.where(northern, jnp.where(odd, two, one), sides[:LANE])
        wide[top, right:] = jnp.where(northern, jnp.where(odd, one, two), sides[LANE:])


def conv(wide, tap, first, rows, starts, store):
    lines = rows // 2
    chunk = max(1, 32 // lines)

    def parity(q, carry):
        for n in range(0, len(starts), chunk):
            cols = starts[n : n + chunk]
            sums = [[None] * len(cols) for _ in range(lines)]
            for k in range(lines + KERNEL - 1):
                for j in range(KERNEL):
                    at = [BASE + c + DILATION * j for c in cols]
                    values = [wide[first + q + 2 * k, a : a + LANE] for a in at]
                    for i in range(KERNEL):
                        line = k - i
                        if 0 <= line < lines:
                            weight = tap(k, i, j)
                            for g, value in enumerate(values):
                                term, old = weight * value, sums[line][g]
                                sums[line][g] = term if old is None else old + term
            for line in range(lines):
                for g, c in enumerate(cols):
                    store(first + q + 2 * line, c, sums[line][g])
        return carry

    lax.fori_loop(0, 2, parity, 0)


def sea_kernel(mask, sea):
    rows, _, channels = sea.shape
    value = mask[...].astype(BF16)
    at = lax.broadcasted_iota(jnp.int32, (rows, channels), 0)
    for r in range(rows):
        pick = jnp.where(at == r, 1.0, 0.0).astype(BF16)
        row = lax.dot_general(value, pick, (((0,), (0,)), ((), ())), preferred_element_type=F32)
        sea[r] = row.astype(BF16)


def mask_kernel(field, sea, masked):
    masked[...] = field[...] * sea[...]


def rim_fold_kernel(block, flags, facing, near, *rest):
    *rest, far = rest
    rim_kernel(block, flags, facing, near, far)
    fold_kernel(block, flags, far, *rest)


def mask_rim_kernel(field, sea, flags, masked, *rest):
    mask_kernel(field, sea, masked)
    rim_fold_kernel(masked, flags, *rest)


def block_pass(first, rows, blocks, spread, sea, weights, state, arrive=None):
    wide, mixed, result, grad, upstream, up_part, down_part, sums = state
    taps, gain, shift, up, down = weights
    channels = wide.shape[2]
    for k in range(TAPS):
        spread[k] = jnp.broadcast_to(taps[k : k + 1], (LANE, channels))

    def store(row, col, value):
        mixed[row, col : col + LANE] = value

    starts = [c for col, cols in blocks for c in range(col, col + cols, LANE)]
    conv(wide, lambda k, i, j: spread[i * KERNEL + j], first, rows, starts, store)
    width = sum(cols for _, cols in blocks)
    cells = rows * width

    def take(ref, row=0, col=0):
        parts = [ref[first + row : first + row + rows, col + c : col + c + n].astype(F32) for c, n in blocks]
        return jnp.concatenate(parts, 1).reshape(cells, channels)

    def put(ref, value):
        value, at = value.reshape(rows, width, channels), 0
        for c, n in blocks:
            ref[first : first + rows, c : c + n] = value[:, at : at + n].astype(ref.dtype)
            at += n

    up_w, down_w, gain_v = up[...], down[...], gain[...]
    nt = (((1,), (1,)), ((), ()))
    tn = (((0,), (0,)), ((), ()))
    value = take(mixed)
    centered = value - jnp.mean(value, -1, keepdims=True)
    rstd = lax.rsqrt(jnp.mean(centered * centered, -1, keepdims=True) + 1e-06)
    unit = centered * rstd
    normed = (unit * gain_v + shift[...]).astype(BF16)
    pre = jnp.dot(normed, up_w, preferred_element_type=F32)
    square = pre * pre
    tanh = jnp.tanh(pre * (SLOPE + (SLOPE * CUBIC) * square))
    gate = 0.5 + 0.5 * tanh
    activated = (pre * gate).astype(BF16)
    product = jnp.dot(activated, down_w, preferred_element_type=F32)
    ocean = take(sea)
    put(result, (take(wide, REACH, LEFT) + product) * ocean)
    if arrive is not None:
        arrive()
    above = (take(upstream) * ocean).astype(BF16)
    down_part[...] += lax.dot_general(above, activated, tn, preferred_element_type=F32)
    act_grad = lax.dot_general(above, down_w, nt, preferred_element_type=F32)
    deriv = gate + pre * (gate * (1.0 - tanh)) * (SLOPE + (3.0 * SLOPE * CUBIC) * square)
    pre_grad = (act_grad * deriv).astype(BF16)
    up_part[...] += lax.dot_general(normed, pre_grad, tn, preferred_element_type=F32)
    norm_in = lax.dot_general(pre_grad, up_w, nt, preferred_element_type=F32)
    sums[0] += jnp.sum((norm_in * unit).reshape(cells // LANE, LANE, channels), 0)
    sums[1] += jnp.sum(norm_in.reshape(cells // LANE, LANE, channels), 0)
    scaled = norm_in * gain_v
    inner = jnp.mean(scaled * unit, -1, keepdims=True)
    moved = rstd * (scaled - jnp.mean(scaled, -1, keepdims=True) - unit * inner)
    put(mixed, moved)
    put(grad, moved)


STATE = 8


def lower_kernel(block, below, cotangent, sea, flags, *refs):
    weights, state, (spread, sem) = refs[:5], refs[5:-2], refs[-2:]
    rows, cols = block.shape[0], block.shape[1]
    upstream, up_part, down_part, sums = state[4:]
    fetch = pltpu.make_async_copy(cotangent, upstream, sem)
    fetch.start()
    for ref in (up_part, down_part, sums):
        ref[...] = jnp.zeros_like(ref)
    fill_own(state[0], flags, block, below)
    block_pass(0, rows // 2, [(LANE, cols - 2 * LANE)], spread, sea, weights, state, fetch.wait)


def upper_kernel(*refs):
    above, folded, sea, flags = refs[STATE : STATE + 4]
    weights, state, spread = refs[STATE + 4 : STATE + 9], refs[STATE + 9 : -1], refs[-1]
    rows, cols = sea.shape[0], sea.shape[1]
    fill_top(state[0], flags, above, folded)
    block_pass(rows // 2, rows // 2, [(LANE, cols - 2 * LANE)], spread, sea, weights, state)


def edge_kernel(*refs):
    sides, sea, flags = refs[STATE : STATE + 6], refs[STATE + 6], refs[STATE + 7]
    weights, state, (mine, other, spread) = refs[STATE + 8 : STATE + 13], refs[STATE + 13 : -3], refs[-3:]
    rows, cols = sea.shape[0], sea.shape[1]
    hidden, channels = mine.shape
    fill_sides(state[0], flags, *sides)
    block_pass(0, rows, [(0, LANE), (cols - LANE, LANE)], spread, sea, weights, state)
    up_part, down_part = state[5:7]
    down_sum = down_part[...].T
    up_sum = jnp.concatenate([up_part[:, n : n + channels] for n in range(0, hidden, channels)], 0)
    odd = on(flags, CORE)
    mine[...] = jnp.where(odd, up_sum, down_sum)
    other[...] = jnp.where(odd, down_sum, up_sum).astype(BF16)


def kernel_kernel(wide, mixed, result, norm, output, small_out, sem):
    rows, cols, channels = mixed.shape
    send = pltpu.make_async_copy(result, output, sem)
    send.start()
    small = jnp.zeros((LANE, channels), F32)
    pieces = []
    for taps_i in (range(0, 4), range(4, KERNEL)):

        def quad(n, sums, taps_i=taps_i):
            base = (n // 2) * 8 + n % 2
            sums = list(sums)
            for g in range(cols // LANE):
                grads = [mixed[base + 2 * m, g * LANE : (g + 1) * LANE] for m in range(4)]
                for k in range(taps_i[0], taps_i[-1] + 4):
                    for j in range(KERNEL):
                        a = BASE + g * LANE + DILATION * j
                        value = wide[base + 2 * k, a : a + LANE]
                        for m in range(4):
                            if k - m in taps_i:
                                at = (k - m - taps_i[0]) * KERNEL + j
                                sums[at] = sums[at] + grads[m] * value
            return tuple(sums)

        zero = tuple(small for _ in range(len(taps_i) * KERNEL))
        pieces += list(lax.fori_loop(0, rows // 4, quad, zero))
    pieces += [norm[0], norm[1]]
    pieces = [jnp.sum(p, 0, keepdims=True) for p in pieces]
    pieces += [jnp.zeros((small_out.shape[0] - TAPS - 2, channels), F32)]
    small_out[...] = jnp.concatenate(pieces, 0)
    send.wait()


def final_kernel(total, back, flags, kernel_grad, norm_grad, up_grad, down_grad, *, factor):
    hidden, channels = down_grad.shape
    odd = on(flags, CORE)
    own, theirs = total[:hidden] * factor, back[:hidden] * factor
    down_grad[...] = jnp.where(odd, theirs, own)
    up = jnp.where(odd, own, theirs)
    for n in range(hidden // channels):
        up_grad[:, n * channels : (n + 1) * channels] = up[n * channels : (n + 1) * channels]
    small = (total[hidden:] + back[hidden:]) * factor
    kernel_grad[...] = small[:TAPS]
    norm_grad[...] = small[TAPS : TAPS + 2]


def backward_kernel(block, below, above, folded, far, near, own, corner, low, high, cotangent, sea, taps, flags,
                    field_grad, token, wide, spread, upper):
    rows, cols, channels = block.shape
    northern = on(flags, NORTHERN)
    for k in range(TAPS):
        flipped = jnp.broadcast_to(taps[TAPS - 1 - k : TAPS - k], (LANE, channels))
        plain = jnp.broadcast_to(taps[k : k + 1], (LANE, channels))
        spread[k] = flipped
        upper[k] = jnp.where(northern, plain, flipped)
    fill_own(wide, flags, block, below)
    fill_top(wide, flags, above, folded)
    fill_sides(wide, flags, far, near, own, corner, low, high)
    edge = (REACH + rows) // 2

    def tap(k, i, j):
        return (upper if k >= edge else spread)[i * KERNEL + j]

    def store(row, col, value):
        at = (row, slice(col, col + LANE))
        field_grad[at] = ((cotangent[at].astype(F32) + value) * sea[at].astype(F32)).astype(BF16)

    conv(wide, tap, 0, rows, list(range(0, cols, LANE)), store)
    token[...] = jnp.zeros_like(token)


def call(kernel, outs, operands, scratch=(), far=(), far_outs=(), aliases=(), work=0, name=None):
    vmem, hbm = pl.BlockSpec(memory_space=pltpu.VMEM), pl.BlockSpec(memory_space=pltpu.HBM)
    moved = sum(math.prod(a.shape) * a.dtype.itemsize for a in (*operands, *outs))
    return pl.pallas_call(
        kernel,
        out_shape=outs,
        in_specs=[hbm if n in far else vmem for n in range(len(operands))],
        out_specs=[hbm if n in far_outs else vmem for n in range(len(outs))],
        scratch_shapes=scratch,
        input_output_aliases=dict(aliases),
        compiler_params=pltpu.CompilerParams(vmem_limit_bytes=24 * 1024 * 1024),
        cost_estimate=pl.CostEstimate(flops=work, bytes_accessed=moved, transcendentals=0),
        name=name,
    )(*operands)


def shards(field, cotangent, land_mask, kernel_taps, norm_gain, norm_shift, up_weight, down_weight):
    rows, cols, channels = field.shape[1:]
    hidden = up_weight.shape[1]
    shape = jax.ShapeDtypeStruct
    tile = (rows, cols, channels)
    flags = flags_of()
    (sea,) = call(sea_kernel, (shape(tile, BF16),), (land_mask,), work=2 * 10**9, name="sea")
    masked, below, above, folded, far, near, own, corner, low, high = extend(field[0], sea, flags)
    wide = (rows + 2 * REACH, cols + 2 * LEFT, channels)
    spread = pltpu.VMEM((TAPS, LANE, channels), F32)
    large, small = (hidden, channels), (64, channels)
    weights = (kernel_taps, norm_gain[None], norm_shift[None], up_weight, down_weight)
    part = shape((channels, hidden), F32)
    state = (shape(wide, F32), shape(tile, F32), shape(tile, BF16), shape(tile, BF16), shape(tile, BF16), part, part, shape((2, LANE, channels), F32))
    same = tuple((n, n) for n in range(STATE))
    passed = call(
        lower_kernel,
        state,
        (masked, below, cotangent[0], sea, flags, *weights),
        [spread, pltpu.SemaphoreType.DMA],
        far=(2,),
        work=LOWER_WORK,
        name="lower",
    )
    passed = call(upper_kernel, state, (*passed, above, folded, sea, flags, *weights), [spread], aliases=same, work=UPPER_WORK, name="upper")
    *passed, mine, other = call(
        edge_kernel,
        (*state, shape(large, F32), shape(large, BF16)),
        (*passed, far, near, own, corner, low, high, sea, flags, *weights),
        [spread],
        aliases=same,
        work=10**9,
        name="edge",
    )
    widened, mixed_grad, result, grad, upstream, _, _, sums = passed
    core, rest = stages()
    received = partners(other, core)
    output, last_sums = call(
        kernel_kernel,
        (shape(tile, BF16), shape(small, F32)),
        (widened, mixed_grad, result, sums),
        [pltpu.SemaphoreType.DMA],
        far_outs=(0,),
        work=KERNEL_WORK,
        name="kernel_gradient",
    )
    joined = shape((hidden + small[0], channels), BF16)
    if is_pairs():
        block_halo = round_one(rim_fold_kernel, (grad, flags), grad)
        (sent,) = call(join_kernel, (joined,), (mine, received, last_sums, block_halo[JOIN_TOKEN]), name="join")
        values = stage(sent, rest[0])
        halo = round_two(block_halo, flags)
    else:
        (sent,) = call(join_kernel, (joined,), (mine, received, last_sums), name="join")
        values = stage(sent, rest[0])
        halo = extend_any(grad)
    for pair in rest[1:]:
        (sent,) = call(add_kernel, (shape(sent.shape, BF16),), (*values, halo[0]), name="add")
        values = stage(sent, pair)
    field_grad, token = call(
        backward_kernel,
        (shape(tile, BF16), shape((LANE, channels), F32)),
        (grad, *halo, upstream, sea, kernel_taps, flags),
        [pltpu.VMEM(wide, F32), spread, spread],
        work=3 * 10**9,
        name="backward",
    )
    (total,) = call(add_kernel, (shape(joined.shape, F32),), (*values, token), name="add")
    back = partners(total, core)
    count = rows * cols * lax.axis_size("lon") * lax.axis_size("lat") * lax.axis_size("ens")
    kernel_grad, norm_grad, up_grad, down_grad = call(
        functools.partial(final_kernel, factor=1.0 / math.sqrt(count)),
        (shape((TAPS, channels), F32), shape((2, channels), F32), shape((channels, hidden), F32), shape((hidden, channels), F32)),
        (total, back, flags),
        name="final",
    )
    return output[None], field_grad[None], kernel_grad, norm_grad, up_grad, down_grad


def solution(mesh):
    grid = P("ens", "lat", "lon", None)
    return jax.shard_map(
        shards,
        mesh=mesh,
        in_specs=(grid, grid, P("lat", "lon"), P(), P(), P(), P(), P()),
        out_specs=(grid, grid, P(), P(), P(), P()),
        check_vma=False,
    )
```

```python
import functools
import math

import jax
import jax.numpy as jnp
from jax import lax
from jax.experimental import pallas as pl
from jax.experimental.pallas import tpu as pltpu
from jax.sharding import PartitionSpec as P

KERNEL = 7
DILATION = 2
REACH = 6
TAPS = KERNEL * KERNEL
LANE = 8
LEFT = 8
BASE = LEFT - REACH
LOWER_WORK, UPPER_WORK, KERNEL_WORK = 10**8, 2 * 10**9, 10**8
SLOPE = math.sqrt(2.0 / math.pi)
CUBIC = 0.044715
F32, BF16 = jnp.float32, jnp.bfloat16


def route(axes, target):
    sizes = [lax.axis_size(a) for a in axes]
    pairs = []
    for flat in range(math.prod(sizes)):
        rest, at = flat, []
        for size in reversed(sizes):
            at.append(rest % size)
            rest //= size
        at = at[::-1]
        to = target(*at)
        if to is not None:
            dest = 0
            for size, i in zip(sizes, to):
                dest = dest * size + i
            pairs.append((flat, dest))
    return pairs


def is_northern():
    return lax.axis_index("lat") == lax.axis_size("lat") - 1


def xor_partner(value, axis, bits):
    return lax.ppermute(value, axis, [(i, i ^ bits) for i in range(lax.axis_size(axis))])


JOIN_TOKEN = 3
NORTHERN, ODD, INNER, CORE = range(4)


def flags_of():
    odd = lax.axis_index("lon") % 2 if lax.axis_size("lon") == 4 else 0
    values = (is_northern(), odd, lax.axis_index("lat") > 0, lax.axis_index("ens") % 2)
    row = lax.broadcasted_iota(jnp.int32, (LANE, 128), 0)
    return sum(jnp.where(row == n, jnp.asarray(v, jnp.int32), 0) for n, v in enumerate(values))


def on(flags, n):
    return flags[n : n + 1] == 1


def rim_kernel(block, flags, facing, near, far):
    rows, cols = block.shape[0], block.shape[1]
    northern, odd = on(flags, NORTHERN), on(flags, ODD)
    for k in range(REACH):
        low, high = block[k].astype(F32), block[rows - REACH + k].astype(F32)
        facing[k] = jnp.where(northern, low, high).astype(BF16)
    for r in range(rows):
        head = block[r, : 2 * LANE].astype(F32)[:LANE]
        tail = block[r, cols - 2 * LANE :].astype(F32)[LANE:]
        near[r] = jnp.where(odd, head, tail).astype(BF16)
        far[r] = jnp.where(odd, tail, head).astype(BF16)


def fold_kernel(block, flags, far, *refs):
    joint, corner, own = refs[-3:]
    rows, cols, channels = block.shape
    start = rows * LANE
    odd = on(flags, ODD)
    down = lax.broadcasted_iota(jnp.int32, (cols, cols), 0)
    across = lax.broadcasted_iota(jnp.int32, (cols, cols), 1)
    turn = jnp.where(down + across == cols - 1, 1.0, 0.0).astype(BF16)
    joint[:start] = far[...].astype(F32).reshape(start, channels).astype(BF16)
    for k in range(REACH):
        row = jnp.dot(turn, block[rows - 1 - k], preferred_element_type=F32)
        joint[start + k * cols : start + (k + 1) * cols] = row.astype(BF16)
        head, tail = row[:LANE], row[cols - LANE :]
        corner[k] = jnp.where(odd, tail, head).astype(BF16)
        own[k] = jnp.where(odd, head, tail).astype(BF16)


def corner_kernel(near, far, flags, *refs):
    (facing,) = refs[-1:]
    rows = near.shape[0]
    northern, odd = on(flags, NORTHERN), on(flags, ODD)
    for k in range(REACH):
        one, two = (
            jnp.where(northern, a[k].astype(F32), a[rows - REACH + k].astype(F32)) for a in (far, near)
        )
        sides = [jnp.where(odd, two, one), jnp.where(odd, one, two)]
        facing[k] = jnp.concatenate(sides, 0).astype(BF16)


def is_pairs():
    return (lax.axis_size("lat"), lax.axis_size("lon"), lax.axis_size("ens")) == (2, 4, 4)


def ring(axis, step, closed=True):
    count = lax.axis_size(axis)
    return [(i, (i + step) % count) for i in range(count) if closed or 0 <= i + step < count]


def extend_any(block):
    rows, cols, channels = block.shape
    lons = lax.axis_size("lon")
    top, bottom, flipped = block[rows - REACH :], block[:REACH], block[rows - REACH :][::-1, ::-1]
    west = lax.ppermute(block[:, cols - LANE :], "lon", ring("lon", 1))
    east = lax.ppermute(block[:, :LANE], "lon", ring("lon", -1))
    folded = lax.ppermute(flipped, "lon", [(i, lons - 1 - i) for i in range(lons)])
    left = lax.ppermute(folded[:, cols - LANE :], "lon", ring("lon", 1))
    right = lax.ppermute(folded[:, :LANE], "lon", ring("lon", -1))
    below = lax.ppermute(top, "lat", ring("lat", 1, False))
    above = lax.ppermute(bottom, "lat", ring("lat", -1, False))
    sides = [jnp.concatenate([west[at], east[at]], 1) for at in (slice(rows - REACH, rows), slice(REACH))]
    low = lax.ppermute(sides[0], "lat", ring("lat", 1, False))
    high = lax.ppermute(sides[1], "lat", ring("lat", -1, False))
    return below, above, folded, west, east, left, right, low, high


def shapes_of(block):
    rows, cols, channels = block.shape
    sizes = ((REACH, cols), (rows, LANE), (REACH, LANE), (REACH, 2 * LANE))
    return [jax.ShapeDtypeStruct((*size, channels), BF16) for size in sizes]


def extend(field, sea, flags):
    tile = jax.ShapeDtypeStruct(field.shape, BF16)
    if not is_pairs():
        (block,) = call(mask_kernel, (tile,), (field, sea), name="mask")
        return block, *extend_any(block)
    block, *pieces = round_one(mask_rim_kernel, (field, sea, flags), field, (tile,))
    return block, *round_two(pieces, flags, pieces[4])


def round_one(kernel, operands, block, outs=()):
    strip, side, corner, _ = shapes_of(block)
    both = jax.ShapeDtypeStruct((side.shape[0] * LANE + REACH * strip.shape[1], block.shape[2]), BF16)
    *made, facing, near, both, corner, own = call(
        kernel, (*outs, strip, side, both, corner, corner), operands, [pltpu.VMEM(side.shape, BF16)], work=2 * 10**9, name="rim"
    )
    both, facing = xor_partner(both, "lon", 3), xor_partner(facing, "lat", 1)
    near, corner = xor_partner(near, "lon", 1), xor_partner(corner, "lon", 2)
    return *made, facing, near, both, own, corner


def round_two(pieces, flags, *after):
    facing, near, both, own, corner = pieces
    rows, channels = near.shape[0], near.shape[2]
    cells = rows * LANE
    far, folded = both[:cells].reshape(near.shape), both[cells:].reshape(facing.shape)
    corners = jax.ShapeDtypeStruct((REACH, 2 * LANE, channels), BF16)
    (corners,) = call(corner_kernel, (corners,), (near, far, flags, *after), name="corners")
    corners = xor_partner(corners, "lat", 1)
    return facing, facing, folded, far, near, own, corner, corners, corners


def partners(value, bits):
    axes = tuple(a for a in ("lon", "lat", "ens") if a in [b[0] for b in bits])
    flip = {a: 0 for a in axes}
    for a, b in bits:
        flip[a] ^= b
    return lax.ppermute(value, axes, route(axes, lambda *at: [i ^ flip[a] for a, i in zip(axes, at)]))


def add_kernel(*refs):
    refs[-1][...] = added([ref[...] for ref in refs[:4]]).astype(refs[-1].dtype)


def stages():
    bits = {a: [(a, 1 << b) for b in range(lax.axis_size(a).bit_length() - 1)] for a in ("ens", "lat", "lon")}
    rest = bits["ens"][1:] + bits["lat"] + bits["lon"]
    return bits["ens"][:1], [rest[n : n + 2] for n in range(0, len(rest), 2)]


def stage(sent, pair):
    if len(pair) == 1:
        return [sent, partners(sent, pair)]
    far = partners(sent, pair)
    return [sent, partners(sent, pair[:1]), partners(sent, pair[1:]), far]


def added(values):
    values = [v.astype(F32) for v in values]
    return sum(values) if len(values) == 2 else (values[0] + values[1]) + (values[2] + values[3])


def add_kernel(*refs):
    refs[-1][...] = added([ref[...] for ref in refs[:4]]).astype(refs[-1].dtype)


def join_kernel(mine, core, small, *refs):
    (joined,) = refs[-1:]
    half = mine.shape[0]
    joined[:half] = (mine[...] + core[...].astype(F32)).astype(BF16)
    joined[half:] = small[...].astype(BF16)


def cut_kernel(mine, core, small, flags, token, keep, away):
    quarter, eighth = mine.shape[0] // 2, small.shape[0] // 2
    northern = on(flags, NORTHERN)
    large, little = mine[...] + core[...].astype(F32), small[...]
    for ref, flag in ((keep, northern), (away, jnp.logical_not(northern))):
        ref[:quarter] = jnp.where(flag, large[quarter:], large[:quarter]).astype(BF16)
        ref[quarter:] = jnp.where(flag, little[eighth:], little[:eighth]).astype(BF16)


def gather_kernel(own, core, lat, both, flags, kernel_grad, norm_grad, up_grad, down_grad, *, factor):
    hidden, channels = down_grad.shape
    northern, odd = on(flags, NORTHERN), on(flags, CORE)
    own, core, lat, both = (ref[...].astype(F32) * factor for ref in (own, core, lat, both))
    here = jnp.where(odd, core, own), jnp.where(odd, own, core)
    there = jnp.where(odd, both, lat), jnp.where(odd, lat, both)
    low = [jnp.where(northern, b, a) for a, b in zip(here, there)]
    high = [jnp.where(northern, a, b) for a, b in zip(here, there)]
    quarter = hidden // 2
    down_grad[...] = jnp.concatenate([low[0][:quarter], high[0][:quarter]], 0)
    up = jnp.concatenate([low[1][:quarter], high[1][:quarter]], 0)
    for n in range(hidden // channels):
        up_grad[:, n * channels : (n + 1) * channels] = up[n * channels : (n + 1) * channels]
    small = jnp.concatenate([a[0][quarter:] + a[1][quarter:] for a in (low, high)], 0)
    kernel_grad[...] = small[:TAPS]
    norm_grad[...] = small[TAPS : TAPS + 2]


def fill_own(wide, flags, block, below):
    rows, cols = block.shape[0], block.shape[1]
    inner = on(flags, INNER)
    for r in range(rows):
        wide[REACH + r, LEFT : LEFT + cols] = block[r].astype(F32)
    for k in range(REACH):
        wide[k, LEFT : LEFT + cols] = jnp.where(inner, below[k].astype(F32), 0.0)


def fill_top(wide, flags, above, folded):
    cols = above.shape[1]
    northern = on(flags, NORTHERN)
    for k in range(REACH):
        value = jnp.where(northern, folded[k].astype(F32), above[k].astype(F32))
        wide[wide.shape[0] - REACH + k, LEFT : LEFT + cols] = value


def fill_sides(wide, flags, far, near, own, corner, low, high):
    rows, right = far.shape[0], wide.shape[1] - LEFT
    northern, odd, inner = on(flags, NORTHERN), on(flags, ODD), on(flags, INNER)
    for r in range(rows):
        one, two = far[r].astype(F32), near[r].astype(F32)
        wide[REACH + r, :LEFT] = jnp.where(odd, two, one)
        wide[REACH + r, right:] = jnp.where(odd, one, two)
    for k in range(REACH):
        sides = jnp.where(inner, low[k].astype(F32), 0.0)
        wide[k, :LEFT], wide[k, right:] = sides[:LANE], sides[LANE:]
        sides, one, two = high[k].astype(F32), own[k].astype(F32), corner[k].astype(F32)
        top = REACH + rows + k
        wide[top, :LEFT] = jnp.where(northern, jnp.where(odd, two, one), sides[:LANE])
        wide[top, right:] = jnp.where(northern, jnp.where(odd, one, two), sides[LANE:])


def conv(wide, tap, first, rows, starts, store):
    lines = rows // 2
    chunk = max(1, 32 // lines)

    def parity(q, carry):
        for n in range(0, len(starts), chunk):
            cols = starts[n : n + chunk]
            sums = [[None] * len(cols) for _ in range(lines)]
            for k in range(lines + KERNEL - 1):
                for j in range(KERNEL):
                    at = [BASE + c + DILATION * j for c in cols]
                    values = [wide[first + q + 2 * k, a : a + LANE] for a in at]
                    for i in range(KERNEL):
                        line = k - i
                        if 0 <= line < lines:
                            weight = tap(k, i, j)
                            for g, value in enumerate(values):
                                term, old = weight * value, sums[line][g]
                                sums[line][g] = term if old is None else old + term
            for line in range(lines):
                for g, c in enumerate(cols):
                    store(first + q + 2 * line, c, sums[line][g])
        return carry

    lax.fori_loop(0, 2, parity, 0)


def sea_kernel(mask, sea):
    rows, _, channels = sea.shape
    value = mask[...].astype(BF16)
    at = lax.broadcasted_iota(jnp.int32, (rows, channels), 0)
    for r in range(rows):
        pick = jnp.where(at == r, 1.0, 0.0).astype(BF16)
        row = lax.dot_general(value, pick, (((0,), (0,)), ((), ())), preferred_element_type=F32)
        sea[r] = row.astype(BF16)


def mask_kernel(field, sea, masked):
    masked[...] = field[...] * sea[...]


def rim_fold_kernel(block, flags, facing, near, *rest):
    *rest, far = rest
    rim_kernel(block, flags, facing, near, far)
    fold_kernel(block, flags, far, *rest)


def mask_rim_kernel(field, sea, flags, masked, *rest):
    mask_kernel(field, sea, masked)
    rim_fold_kernel(masked, flags, *rest)


def block_pass(first, rows, blocks, spread, sea, weights, state, arrive=None):
    wide, mixed, result, grad, upstream, up_part, down_part, sums = state
    taps, gain, shift, up, down = weights
    channels = wide.shape[2]
    for k in range(TAPS):
        spread[k] = jnp.broadcast_to(taps[k : k + 1], (LANE, channels))

    def store(row, col, value):
        mixed[row, col : col + LANE] = value

    starts = [c for col, cols in blocks for c in range(col, col + cols, LANE)]
    conv(wide, lambda k, i, j: spread[i * KERNEL + j], first, rows, starts, store)
    width = sum(cols for _, cols in blocks)
    cells = rows * width

    def take(ref, row=0, col=0):
        parts = [ref[first + row : first + row + rows, col + c : col + c + n].astype(F32) for c, n in blocks]
        return jnp.concatenate(parts, 1).reshape(cells, channels)

    def put(ref, value):
        value, at = value.reshape(rows, width, channels), 0
        for c, n in blocks:
            ref[first : first + rows, c : c + n] = value[:, at : at + n].astype(ref.dtype)
            at += n

    up_w, down_w, gain_v = up[...], down[...], gain[...]
    nt = (((1,), (1,)), ((), ()))
    tn = (((0,), (0,)), ((), ()))
    value = take(mixed)
    centered = value - jnp.mean(value, -1, keepdims=True)
    rstd = lax.rsqrt(jnp.mean(centered * centered, -1, keepdims=True) + 1e-06)
    unit = centered * rstd
    normed = (unit * gain_v + shift[...]).astype(BF16)
    pre = jnp.dot(normed, up_w, preferred_element_type=F32)
    square = pre * pre
    tanh = jnp.tanh(pre * (SLOPE + (SLOPE * CUBIC) * square))
    gate = 0.5 + 0.5 * tanh
    activated = (pre * gate).astype(BF16)
    product = jnp.dot(activated, down_w, preferred_element_type=F32)
    ocean = take(sea)
    put(result, (take(wide, REACH, LEFT) + product) * ocean)
    if arrive is not None:
        arrive()
    above = (take(upstream) * ocean).astype(BF16)
    down_part[...] += lax.dot_general(above, activated, tn, preferred_element_type=F32)
    act_grad = lax.dot_general(above, down_w, nt, preferred_element_type=F32)
    deriv = gate + pre * (gate * (1.0 - tanh)) * (SLOPE + (3.0 * SLOPE * CUBIC) * square)
    pre_grad = (act_grad * deriv).astype(BF16)
    up_part[...] += lax.dot_general(normed, pre_grad, tn, preferred_element_type=F32)
    norm_in = lax.dot_general(pre_grad, up_w, nt, preferred_element_type=F32)
    sums[0] += jnp.sum((norm_in * unit).reshape(cells // LANE, LANE, channels), 0)
    sums[1] += jnp.sum(norm_in.reshape(cells // LANE, LANE, channels), 0)
    scaled = norm_in * gain_v
    inner = jnp.mean(scaled * unit, -1, keepdims=True)
    moved = rstd * (scaled - jnp.mean(scaled, -1, keepdims=True) - unit * inner)
    put(mixed, moved)
    put(grad, moved)


STATE = 8


def lower_kernel(block, below, cotangent, sea, flags, *refs):
    weights, state, (spread, sem) = refs[:5], refs[5:-2], refs[-2:]
    rows, cols = block.shape[0], block.shape[1]
    upstream, up_part, down_part, sums = state[4:]
    fetch = pltpu.make_async_copy(cotangent, upstream, sem)
    fetch.start()
    for ref in (up_part, down_part, sums):
        ref[...] = jnp.zeros_like(ref)
    fill_own(state[0], flags, block, below)
    block_pass(0, rows // 2, [(LANE, cols - 2 * LANE)], spread, sea, weights, state, fetch.wait)


def upper_kernel(*refs):
    above, folded, sea, flags = refs[STATE : STATE + 4]
    weights, state, spread = refs[STATE + 4 : STATE + 9], refs[STATE + 9 : -1], refs[-1]
    rows, cols = sea.shape[0], sea.shape[1]
    fill_top(state[0], flags, above, folded)
    block_pass(rows // 2, rows // 2, [(LANE, cols - 2 * LANE)], spread, sea, weights, state)


def edge_kernel(*refs):
    sides, sea, flags = refs[STATE : STATE + 6], refs[STATE + 6], refs[STATE + 7]
    weights, state, (mine, other, spread) = refs[STATE + 8 : STATE + 13], refs[STATE + 13 : -3], refs[-3:]
    rows, cols = sea.shape[0], sea.shape[1]
    hidden, channels = mine.shape
    fill_sides(state[0], flags, *sides)
    block_pass(0, rows, [(0, LANE), (cols - LANE, LANE)], spread, sea, weights, state)
    up_part, down_part = state[5:7]
    down_sum = down_part[...].T
    up_sum = jnp.concatenate([up_part[:, n : n + channels] for n in range(0, hidden, channels)], 0)
    odd = on(flags, CORE)
    mine[...] = jnp.where(odd, up_sum, down_sum)
    other[...] = jnp.where(odd, down_sum, up_sum).astype(BF16)


def kernel_kernel(wide, mixed, result, norm, output, small_out, sem):
    rows, cols, channels = mixed.shape
    send = pltpu.make_async_copy(result, output, sem)
    send.start()
    small = jnp.zeros((LANE, channels), F32)
    pieces = []
    for taps_i in (range(0, 4), range(4, KERNEL)):

        def quad(n, sums, taps_i=taps_i):
            base = (n // 2) * 8 + n % 2
            sums = list(sums)
            for g in range(cols // LANE):
                grads = [mixed[base + 2 * m, g * LANE : (g + 1) * LANE] for m in range(4)]
                for k in range(taps_i[0], taps_i[-1] + 4):
                    for j in range(KERNEL):
                        a = BASE + g * LANE + DILATION * j
                        value = wide[base + 2 * k, a : a + LANE]
                        for m in range(4):
                            if k - m in taps_i:
                                at = (k - m - taps_i[0]) * KERNEL + j
                                sums[at] = sums[at] + grads[m] * value
            return tuple(sums)

        zero = tuple(small for _ in range(len(taps_i) * KERNEL))
        pieces += list(lax.fori_loop(0, rows // 4, quad, zero))
    pieces += [norm[0], norm[1]]
    pieces = [jnp.sum(p, 0, keepdims=True) for p in pieces]
    pieces += [jnp.zeros((small_out.shape[0] - TAPS - 2, channels), F32)]
    small_out[...] = jnp.concatenate(pieces, 0)
    send.wait()


def final_kernel(total, back, flags, kernel_grad, norm_grad, up_grad, down_grad, *, factor):
    hidden, channels = down_grad.shape
    odd = on(flags, CORE)
    own, theirs = total[:hidden] * factor, back[:hidden] * factor
    down_grad[...] = jnp.where(odd, theirs, own)
    up = jnp.where(odd, own, theirs)
    for n in range(hidden // channels):
        up_grad[:, n * channels : (n + 1) * channels] = up[n * channels : (n + 1) * channels]
    small = (total[hidden:] + back[hidden:]) * factor
    kernel_grad[...] = small[:TAPS]
    norm_grad[...] = small[TAPS : TAPS + 2]


def backward_kernel(block, below, above, folded, far, near, own, corner, low, high, cotangent, sea, taps, flags,
                    field_grad, token, wide, spread, upper):
    rows, cols, channels = block.shape
    northern = on(flags, NORTHERN)
    for k in range(TAPS):
        flipped = jnp.broadcast_to(taps[TAPS - 1 - k : TAPS - k], (LANE, channels))
        plain = jnp.broadcast_to(taps[k : k + 1], (LANE, channels))
        spread[k] = flipped
        upper[k] = jnp.where(northern, plain, flipped)
    fill_own(wide, flags, block, below)
    fill_top(wide, flags, above, folded)
    fill_sides(wide, flags, far, near, own, corner, low, high)
    edge = (REACH + rows) // 2

    def tap(k, i, j):
        return (upper if k >= edge else spread)[i * KERNEL + j]

    def store(row, col, value):
        at = (row, slice(col, col + LANE))
        field_grad[at] = ((cotangent[at].astype(F32) + value) * sea[at].astype(F32)).astype(BF16)

    conv(wide, tap, 0, rows, list(range(0, cols, LANE)), store)
    token[...] = jnp.zeros_like(token)


def call(kernel, outs, operands, scratch=(), far=(), far_outs=(), aliases=(), work=0, name=None):
    vmem, hbm = pl.BlockSpec(memory_space=pltpu.VMEM), pl.BlockSpec(memory_space=pltpu.HBM)
    moved = sum(math.prod(a.shape) * a.dtype.itemsize for a in (*operands, *outs))
    return pl.pallas_call(
        kernel,
        out_shape=outs,
        in_specs=[hbm if n in far else vmem for n in range(len(operands))],
        out_specs=[hbm if n in far_outs else vmem for n in range(len(outs))],
        scratch_shapes=scratch,
        input_output_aliases=dict(aliases),
        compiler_params=pltpu.CompilerParams(vmem_limit_bytes=24 * 1024 * 1024),
        cost_estimate=pl.CostEstimate(flops=work, bytes_accessed=moved, transcendentals=0),
        name=name,
    )(*operands)


def shards(field, cotangent, land_mask, kernel_taps, norm_gain, norm_shift, up_weight, down_weight):
    rows, cols, channels = field.shape[1:]
    hidden = up_weight.shape[1]
    shape = jax.ShapeDtypeStruct
    tile = (rows, cols, channels)
    flags = flags_of()
    (sea,) = call(sea_kernel, (shape(tile, BF16),), (land_mask,), work=2 * 10**9, name="sea")
    masked, below, above, folded, far, near, own, corner, low, high = extend(field[0], sea, flags)
    wide = (rows + 2 * REACH, cols + 2 * LEFT, channels)
    spread = pltpu.VMEM((TAPS, LANE, channels), F32)
    large, small = (hidden, channels), (64, channels)
    weights = (kernel_taps, norm_gain[None], norm_shift[None], up_weight, down_weight)
    part = shape((channels, hidden), F32)
    state = (shape(wide, F32), shape(tile, F32), shape(tile, BF16), shape(tile, BF16), shape(tile, BF16), part, part, shape((2, LANE, channels), F32))
    same = tuple((n, n) for n in range(STATE))
    passed = call(
        lower_kernel,
        state,
        (masked, below, cotangent[0], sea, flags, *weights),
        [spread, pltpu.SemaphoreType.DMA],
        far=(2,),
        work=LOWER_WORK,
        name="lower",
    )
    passed = call(upper_kernel, state, (*passed, above, folded, sea, flags, *weights), [spread], aliases=same, work=UPPER_WORK, name="upper")
    *passed, mine, other = call(
        edge_kernel,
        (*state, shape(large, F32), shape(large, BF16)),
        (*passed, far, near, own, corner, low, high, sea, flags, *weights),
        [spread],
        aliases=same,
        work=10**9,
        name="edge",
    )
    widened, mixed_grad, result, grad, upstream, _, _, sums = passed
    core, rest = stages()
    received = partners(other, core)
    output, last_sums = call(
        kernel_kernel,
        (shape(tile, BF16), shape(small, F32)),
        (widened, mixed_grad, result, sums),
        [pltpu.SemaphoreType.DMA],
        far_outs=(0,),
        work=KERNEL_WORK,
        name="kernel_gradient",
    )
    grads = (shape((TAPS, channels), F32), shape((2, channels), F32), shape((channels, hidden), F32), shape((hidden, channels), F32))
    count = rows * cols * lax.axis_size("lon") * lax.axis_size("lat") * lax.axis_size("ens")
    factor = 1.0 / math.sqrt(count)

    def backward(halo):
        return call(
            backward_kernel,
            (shape(tile, BF16), shape((LANE, channels), F32)),
            (grad, *halo, upstream, sea, kernel_taps, flags),
            [pltpu.VMEM(wide, F32), spread, spread],
            work=3 * 10**9,
            name="backward",
        )

    if is_pairs():
        pieces = round_one(rim_fold_kernel, (grad, flags), grad)
        part = shape(((hidden + small[0]) // 2, channels), BF16)
        keep, away = call(cut_kernel, (part, part), (mine, received, last_sums, flags, pieces[JOIN_TOKEN]), name="cut")
        y, x = rest[0]
        values = [keep, partners(keep, [y]), partners(away, [x]), partners(away, [y, x])]
        halo = round_two(pieces, flags)
        (total,) = call(add_kernel, (part,), (*values, halo[0]), name="add")
        values = stage(total, rest[1])
        field_grad, token = backward(halo)
        (total,) = call(add_kernel, (part,), (*values, token), name="add")
        over_lat, size = partners(total, [x]), total.shape[0]
        both = partners(jnp.concatenate([total, over_lat]), core)
        parts = (total, both[:size], over_lat, both[size:])
        weight_grads = call(functools.partial(gather_kernel, factor=factor), grads, (*parts, flags), name="final")
    else:
        joined = shape((hidden + small[0], channels), BF16)
        (total,) = call(join_kernel, (joined,), (mine, received, last_sums), name="join")
        for pair in rest:
            values = stage(total.astype(BF16), pair)
            total = added(values)
        weight_grads = call(
            functools.partial(final_kernel, factor=factor), grads, (total, partners(total, core), flags), name="final"
        )
        field_grad, _ = backward(extend_any(grad))
    kernel_grad, norm_grad, up_grad, down_grad = weight_grads
    return output[None], field_grad[None], kernel_grad, norm_grad, up_grad, down_grad


def solution(mesh):
    grid = P("ens", "lat", "lon", None)
    return jax.shard_map(
        shards,
        mesh=mesh,
        in_specs=(grid, grid, P("lat", "lon"), P(), P(), P(), P(), P()),
        out_specs=(grid, grid, P(), P(), P(), P()),
        check_vma=False,
    )
```
